128 devices in a mesh: rows: 2 (over core), vocab: 64 (over z, y, x).
Axes of the slice: x: 4, y: 4, z: 4, core: 2. Of those that a mesh axis runs over, the one named last changes fastest.
Arguments:
- hidden_states: bfloat16 [512, 2048], P('rows'), may hold values from -30 to 30
- head_weight: bfloat16 [2048, 155648], P('rows', 'vocab'), may hold values from -2.5 to 2.5
- target_logits: bfloat16 [512, 155648], P('rows', 'vocab'), may hold values from -40 to 330
Outputs:
- divergence: float32 [512], P('rows')
- hidden_grad: float32 [512, 2048], P('rows')
- head_grad: float32 [2048, 155648], P('rows', 'vocab')
The draws below stay inside these ranges and needn't reach their ends.
All inputs are finite; a program needn't handle non-finite values.
Results may differ from the reference program's by a relative error of at most 0.0044.
Values may be sent and summed in bfloat16 or wider, within the bound.
No kernel may reach another device: no remote copies, remote signals or barrier semaphores. Data moves between devices by JAX's collectives and lax.ppermute only.
A program may use at most 128 MiB of HBM per device.

```python
import math
import jax
import jax.numpy as jnp
from jax import lax

D = 2048
TOK_DEV = 256
VOCAB = 155648
TOKENS = 512
N_ROWS = 2


def head_matrix(key):
    normal = jax.random.normal(jax.random.fold_in(key, 11), (D, VOCAB), jnp.float32)
    return jnp.clip(normal, -6.0, 6.0) * (3.0 / math.sqrt(D))


def draw_head_weight(key, part):
    return head_matrix(key).astype(jnp.bfloat16)


def draw_hidden_states(key, part):
    own = jax.random.fold_in(key, 3)
    normal = jax.random.normal(own, (TOKENS, D), jnp.float32)
    return jnp.clip(normal, -6.0, 6.0).astype(jnp.bfloat16)


def draw_target_logits(key, part):
    own = jax.random.fold_in(key, 5)
    normal = jax.random.normal(own, (TOKENS, VOCAB), jnp.float32)
    return (jnp.clip(normal, -6.0, 6.0) * 3.0).astype(jnp.bfloat16)


def setup_inputs(seed: int = 0) -> dict:
    seeds = jax.random.split(jax.random.key(seed), 4)
    hidden_states = draw_hidden_states(jax.random.fold_in(seeds[3], 71), 0)
    head_weight = draw_head_weight(jax.random.fold_in(seeds[3], 71), 0)
    target_logits = draw_target_logits(jax.random.fold_in(seeds[3], 71), 0)
    return {"hidden_states": hidden_states, "head_weight": head_weight, "target_logits": target_logits}


def reference(hidden_states, head_weight, target_logits):
    draft = jnp.dot(hidden_states, head_weight, preferred_element_type=jnp.float32)
    target = target_logits.astype(jnp.float32)
    top_t = jnp.max(target, axis=1, keepdims=True)
    lse_target = top_t + jnp.log(jnp.sum(jnp.exp(target - top_t), axis=1, keepdims=True))
    top_q = jnp.max(draft, axis=1, keepdims=True)
    lse_draft = top_q + jnp.log(jnp.sum(jnp.exp(draft - top_q), axis=1, keepdims=True))
    probs_t = jnp.exp(target - lse_target)
    probs_q = jnp.exp(draft - lse_draft)
    divergence = jnp.sum(probs_t * (target - draft), axis=1) - lse_target[:, 0] + lse_draft[:, 0]
    dlogits = ((probs_q - probs_t) * (VOCAB / 1024.0)).astype(jnp.bfloat16)
    hidden_grad = jnp.dot(dlogits, head_weight.T, preferred_element_type=jnp.float32)

    def group_term(total, index):
        start = (index * TOK_DEV).astype(jnp.int32)
        rows_h = lax.dynamic_slice_in_dim(hidden_states, start, TOK_DEV, 0)
        rows_g = lax.dynamic_slice_in_dim(dlogits, start, TOK_DEV, 0)
        term = jnp.dot(rows_h.T, rows_g, preferred_element_type=jnp.float32)
        return total + term, None

    head_grad, _ = lax.scan(group_term, jnp.zeros((D, VOCAB), jnp.float32), jnp.arange(N_ROWS, dtype=jnp.int32))
    return divergence, hidden_grad, head_grad
```

```python
import jax
import jax.numpy as jnp
from jax import lax
from jax.sharding import PartitionSpec as P

SWAP = ((0, 1), (1, 0))


def dot(a, b, ca, cb):
    return lax.dot_general(a, b, (((ca,), (cb,)), ((), ())), preferred_element_type=jnp.float32)


def swap(x):
    return lax.ppermute(x, "rows", SWAP)


def to_all(x, n):
    return lax.all_to_all(jnp.broadcast_to(x[None], (n,) + x.shape), "vocab", 0, 0)


def shards(hidden, weight, target_logits):
    n = lax.axis_size("vocab")
    row = lax.axis_index("rows")
    tokens, width = hidden.shape
    half = weight.shape[0]
    vocab = target_logits.shape[1]

    with jax.named_scope("swap_weight"):
        weight_o = swap(weight)
    mine = lax.dynamic_slice_in_dim(hidden, row * half, half, 1)
    theirs = lax.dynamic_slice_in_dim(hidden, (1 - row) * half, half, 1)
    with jax.named_scope("swap_hidden"):
        mine_o = swap(theirs)

    with jax.named_scope("draft"):
        draft = dot(mine, weight, 1, 0) + dot(theirs, weight_o, 1, 0)

    with jax.named_scope("stats"):
        target = target_logits.astype(jnp.float32)
        peak_t = jnp.max(target, axis=1)
        peak_q = jnp.max(draft, axis=1)
        exp_t = jnp.exp(target - peak_t[:, None])
        part = jnp.stack(
            [
                peak_t,
                jnp.sum(exp_t, axis=1),
                jnp.sum(exp_t * (target - draft), axis=1),
                peak_q,
                jnp.sum(jnp.exp(draft - peak_q[:, None]), axis=1),
            ]
        )
    with jax.named_scope("share_stats"):
        parts = to_all(part, n)
    with jax.named_scope("merge_stats"):
        top_t = jnp.max(parts[:, 0], axis=0)
        top_q = jnp.max(parts[:, 3], axis=0)
        scale_t = jnp.exp(parts[:, 0] - top_t)
        scale_q = jnp.exp(parts[:, 3] - top_q)
        sum_t = jnp.sum(parts[:, 1] * scale_t, axis=0)
        cross = jnp.sum(parts[:, 2] * scale_t, axis=0)
        sum_q = jnp.sum(parts[:, 4] * scale_q, axis=0)
        lse_t = top_t + jnp.log(sum_t)
        lse_q = top_q + jnp.log(sum_q)
        divergence = cross / sum_t - lse_t + lse_q

    with jax.named_scope("dlogits"):
        factor = vocab * n / 1024.0
        p = jnp.exp(target - lse_t[:, None])
        q = jnp.exp(draft - lse_q[:, None])
        dlogits = ((q - p) * factor).astype(jnp.bfloat16)
    with jax.named_scope("swap_dlogits"):
        dlogits_o = swap(dlogits)

    with jax.named_scope("hidden_grad"):
        back = jnp.concatenate([dot(dlogits, weight, 1, 1), dot(dlogits, weight_o, 1, 1)], axis=1)
        back = back.astype(jnp.bfloat16).reshape(n, tokens // n, width)
    with jax.named_scope("scatter_sum"):
        terms = lax.all_to_all(back, "vocab", 0, 0)
    with jax.named_scope("sum"):
        total = jnp.sum(terms.astype(jnp.float32), axis=0)
        total = jnp.roll(total, row * half, axis=1).astype(jnp.bfloat16)
    with jax.named_scope("gather"):
        hidden_grad = to_all(total, n).reshape(tokens, width).astype(jnp.float32)

    with jax.named_scope("head_grad"):
        head_grad = dot(mine, dlogits, 0, 0) + dot(mine_o, dlogits_o, 0, 0)
    return (divergence, hidden_grad, head_grad)


def solution(mesh):
    return jax.shard_map(
        shards,
        mesh=mesh,
        in_specs=(P("rows", None), P("rows", "vocab"), P("rows", "vocab")),
        out_specs=(P("rows"), P("rows", None), P("rows", "vocab")),
        check_vma=False,
    )
```

```python
import functools
import jax
import jax.numpy as jnp
from jax import lax
from jax.experimental import pallas as pl
from jax.experimental.pallas import tpu as pltpu
from jax.sharding import PartitionSpec as P

SWAP = ((0, 1), (1, 0))
TOKENS_PIECE = 16
COLS_PIECE = 512
BLOCK = 640
LIMIT = 40 * 1024 * 1024
F32, BF16 = jnp.float32, jnp.bfloat16


def dot(a, b, ca, cb):
    return lax.dot_general(a, b, (((ca,), (cb,)), ((), ())), preferred_element_type=F32)


def swap(x):
    return lax.ppermute(x, "rows", SWAP)


def params(**kw):
    return pltpu.CompilerParams(vmem_limit_bytes=LIMIT, **kw)


def whole(shape):
    return pl.BlockSpec(shape, lambda *_: (0,) * len(shape))


def lanes_to_rows(columns):
    lane = lax.broadcasted_iota(jnp.int32, (columns[0].shape[0], 128), 1)
    packed = jnp.zeros(lane.shape, F32)
    for i, column in enumerate(columns):
        packed = jnp.where(lane == i, column, packed)
    return packed.T[:8]


def running(first, peak_ref, sum_ref, values):
    peak = jnp.max(values, axis=1, keepdims=True)
    old = jnp.where(first, peak, peak_ref[...])
    new = jnp.maximum(old, peak)
    kept = jnp.where(first, 0.0, sum_ref[...])
    sum_ref[...] = kept * jnp.exp(old - new) + jnp.sum(jnp.exp(values - new), axis=1, keepdims=True)
    peak_ref[...] = new


def own_kernel(vocab, mine, weight, target, acc, stat, peak, total):
    j = pl.program_id(0)
    acc[...] = dot(mine[...], weight[...], 1, 0)
    inside = j * BLOCK + lax.broadcasted_iota(jnp.int32, target.shape, 1) < vocab
    running(j == 0, peak, total, jnp.where(inside, target[...].astype(F32), -jnp.inf))

    @pl.when(j == pl.num_programs(0) - 1)
    def _():
        lane = lax.broadcasted_iota(jnp.int32, stat.shape, 1)
        stat[...] = jnp.where(lane == 0, peak[...], total[...])


def own_part(mine, weight, target):
    tokens, half = mine.shape
    vocab = target.shape[1]
    column = lambda j: (0, j)
    return pl.pallas_call(
        functools.partial(own_kernel, vocab),
        grid=(pl.cdiv(vocab, BLOCK),),
        in_specs=[
            whole((tokens, half)),
            pl.BlockSpec((half, BLOCK), column),
            pl.BlockSpec((tokens, BLOCK), column),
        ],
        out_specs=[pl.BlockSpec((tokens, BLOCK), column), whole((tokens, 128))],
        out_shape=[
            jax.ShapeDtypeStruct((tokens, vocab), F32),
            jax.ShapeDtypeStruct((tokens, 128), F32),
        ],
        scratch_shapes=[pltpu.VMEM((tokens, 1), F32)] * 2,
        compiler_params=params(),
        cost_estimate=pl.CostEstimate(flops=2 * tokens * half * vocab, bytes_accessed=2 * half * vocab, transcendentals=0),
        name="own_part",
    )(mine, weight, target)


def draft_kernel(vocab, theirs, weight, acc, target, stat, draft, out, peak, total, cross):
    j = pl.program_id(0)
    first = j == 0
    value = acc[...] + dot(theirs[...], weight[...], 1, 0)
    draft[...] = value
    inside = j * BLOCK + lax.broadcasted_iota(jnp.int32, target.shape, 1) < vocab
    running(first, peak, total, jnp.where(inside, value, -jnp.inf))
    wide = target[...].astype(F32)
    term = jnp.where(inside, jnp.exp(wide - stat[:, :1]) * (wide - value), 0.0)
    cross[...] = jnp.where(first, 0.0, cross[...]) + jnp.sum(term, axis=1, keepdims=True)

    @pl.when(j == pl.num_programs(0) - 1)
    def _():
        out[...] = lanes_to_rows([stat[:, :1], stat[:, 1:2], cross[...], peak[...], total[...]])


def draft_part(theirs, weight, acc, target, stat):
    tokens, half = theirs.shape
    vocab = target.shape[1]
    column = lambda j: (0, j)
    return pl.pallas_call(
        functools.partial(draft_kernel, vocab),
        grid=(pl.cdiv(vocab, BLOCK),),
        in_specs=[
            whole((tokens, half)),
            pl.BlockSpec((half, BLOCK), column),
            pl.BlockSpec((tokens, BLOCK), column),
            pl.BlockSpec((tokens, BLOCK), column),
            whole((tokens, 128)),
        ],
        out_specs=[pl.BlockSpec((tokens, BLOCK), column), whole((8, tokens))],
        out_shape=[
            jax.ShapeDtypeStruct((tokens, vocab), F32),
            jax.ShapeDtypeStruct((8, tokens), F32),
        ],
        scratch_shapes=[pltpu.VMEM((tokens, 1), F32)] * 3,
        compiler_params=params(),
        cost_estimate=pl.CostEstimate(flops=2 * tokens * half * vocab, bytes_accessed=2 * half * vocab, transcendentals=0),
        name="draft_part",
    )(theirs, weight, acc, target, stat)


def back_kernel(factor, row, parts, draft, target, weight, weight_o, divergence, dlogits, out, buffer, sems):
    half = weight.shape[0]
    per = half // COLS_PIECE
    copies = []
    for j in range(2 * per):
        source = (weight, weight_o)[j // per].at[pl.ds(j % per * COLS_PIECE, COLS_PIECE)]
        copies.append(pltpu.make_async_copy(source, buffer.at[j], sems.at[j]))
        copies[-1].start()

    peaks_t, peaks_q = parts[:, 0, :], parts[:, 3, :]
    top_t = jnp.max(peaks_t, axis=0, keepdims=True)
    top_q = jnp.max(peaks_q, axis=0, keepdims=True)
    scale_t, scale_q = jnp.exp(peaks_t - top_t), jnp.exp(peaks_q - top_q)
    sum_t = jnp.sum(parts[:, 1, :] * scale_t, axis=0, keepdims=True)
    cross = jnp.sum(parts[:, 2, :] * scale_t, axis=0, keepdims=True)
    sum_q = jnp.sum(parts[:, 4, :] * scale_q, axis=0, keepdims=True)
    lse_t, lse_q = top_t + jnp.log(sum_t), top_q + jnp.log(sum_q)
    divergence[...] = cross / sum_t - lse_t + lse_q
    tokens = lse_t.shape[1]
    line = lax.broadcasted_iota(jnp.int32, (128, tokens), 0)
    turned = jnp.where(line == 0, lse_t, lse_q).T
    lse_t, lse_q = turned[:, :1], turned[:, 1:2]

    probs_q = jnp.exp(draft[...] - lse_q)
    probs_t = jnp.exp(target[...].astype(F32) - lse_t)
    dlogits[...] = ((probs_q - probs_t) * factor).astype(BF16)

    for j in range(2 * per):
        copies[j].wait()
        block = dot(dlogits[...], buffer[j], 1, 1).astype(BF16)
        place = lax.rem(row[0] * per + j, 2 * per)
        for i in range(tokens // TOKENS_PIECE):
            out[i * 2 * per + place] = block[i * TOKENS_PIECE : (i + 1) * TOKENS_PIECE]


def back_part(factor, row, parts, draft, target, weight, weight_o):
    tokens, vocab = draft.shape
    half = weight.shape[0]
    n = parts.shape[0]
    pieces = (tokens // TOKENS_PIECE) * (2 * half // COLS_PIECE)
    hbm = pl.BlockSpec(memory_space=pl.ANY)
    vmem = pl.BlockSpec(memory_space=pltpu.VMEM)
    return pl.pallas_call(
        functools.partial(back_kernel, factor),
        in_specs=[pl.BlockSpec(memory_space=pltpu.SMEM), vmem, vmem, vmem, hbm, hbm],
        out_specs=[vmem, vmem, vmem],
        out_shape=[
            jax.ShapeDtypeStruct((1, tokens), F32),
            jax.ShapeDtypeStruct((tokens, vocab), BF16),
            jax.ShapeDtypeStruct((pieces, TOKENS_PIECE, COLS_PIECE), BF16),
        ],
        scratch_shapes=[
            pltpu.VMEM((2 * half // COLS_PIECE, COLS_PIECE, vocab), BF16),
            pltpu.SemaphoreType.DMA((2 * half // COLS_PIECE,)),
        ],
        compiler_params=params(),
        cost_estimate=pl.CostEstimate(flops=4 * tokens * half * vocab, bytes_accessed=4 * half * vocab, transcendentals=0),
        name="back_part",
    )(row, parts, draft, target, weight, weight_o)


def sum_kernel(terms, out):
    total = terms[0].astype(F32)
    for i in range(1, terms.shape[0]):
        total = total + terms[i].astype(F32)
    out[...] = jnp.broadcast_to(total.astype(BF16)[None], out.shape)


def sum_part(terms):
    return pl.pallas_call(
        sum_kernel,
        out_shape=jax.ShapeDtypeStruct(terms.shape, BF16),
        compiler_params=params(),
        name="sum_part",
    )(terms)


def join_kernel(pieces, out):
    across = out.shape[1] // COLS_PIECE
    for i in range(pieces.shape[0]):
        rows = pl.ds(i // across * TOKENS_PIECE, TOKENS_PIECE)
        out[rows, pl.ds(i % across * COLS_PIECE, COLS_PIECE)] = pieces[i].astype(F32)


def join_part(pieces, tokens, width):
    steps = 4
    return pl.pallas_call(
        join_kernel,
        grid=(steps,),
        in_specs=[pl.BlockSpec((pieces.shape[0] // steps,) + pieces.shape[1:], lambda i: (i, 0, 0))],
        out_specs=pl.BlockSpec((tokens // steps, width), lambda i: (i, 0)),
        out_shape=jax.ShapeDtypeStruct((tokens, width), F32),
        compiler_params=params(),
        name="join_part",
    )(pieces)


def shards(hidden, weight, target):
    n = lax.axis_size("vocab")
    row = lax.axis_index("rows")
    tokens, width = hidden.shape
    half, vocab = weight.shape

    with jax.named_scope("swap_weight"):
        weight_o = swap(weight)
    mine = lax.dynamic_slice_in_dim(hidden, row * half, half, 1)
    theirs = lax.dynamic_slice_in_dim(hidden, (1 - row) * half, half, 1)
    with jax.named_scope("swap_hidden"):
        mine_o = swap(theirs)

    acc, stat = own_part(mine, weight, target)
    draft, part = draft_part(theirs, weight_o, acc, target, stat)
    with jax.named_scope("share_stats"):
        parts = lax.all_to_all(jnp.broadcast_to(part[None], (n,) + part.shape), "vocab", 0, 0)
    divergence, dlogits, pieces = back_part(
        vocab * n / 1024.0, jnp.full((1,), row, jnp.int32), parts, draft, target, weight, weight_o
    )
    with jax.named_scope("swap_dlogits"):
        dlogits_o = swap(dlogits)
    with jax.named_scope("scatter_sum"):
        terms = lax.all_to_all(pieces, "vocab", 0, 0)
    totals = sum_part(terms)
    with jax.named_scope("gather"):
        gathered = lax.all_to_all(totals, "vocab", 0, 0)
    hidden_grad = join_part(gathered, tokens, width)

    with jax.named_scope("head_grad"):
        head_grad = dot(mine, dlogits, 0, 0) + dot(mine_o, dlogits_o, 0, 0)
    return (divergence.reshape(tokens), hidden_grad, head_grad)


def solution(mesh):
    return jax.shard_map(
        shards,
        mesh=mesh,
        in_specs=(P("rows", None), P("rows", "vocab"), P("rows", "vocab")),
        out_specs=(P("rows"), P("rows", None), P("rows", "vocab")),
        check_vma=False,
    )
```

```python
import functools
import math
import jax
import jax.numpy as jnp
from jax import lax
from jax.experimental import pallas as pl
from jax.experimental.pallas import tpu as pltpu
from jax.sharding import PartitionSpec as P

SWAP = ((0, 1), (1, 0))
TOKENS_PIECE = 16
COLS_PIECE = 512
BLOCK = 640
LOG2E = math.log2(math.e)
F32, BF16 = jnp.float32, jnp.bfloat16
VMEM = pl.BlockSpec(memory_space=pltpu.VMEM)
HBM = pl.BlockSpec(memory_space=pltpu.HBM)


def dot(a, b, ca, cb):
    return lax.dot_general(a, b, (((ca,), (cb,)), ((), ())), preferred_element_type=F32)


def swap(x):
    return lax.ppermute(x, "rows", SWAP)


def params(mib):
    return pltpu.CompilerParams(vmem_limit_bytes=mib * 1024 * 1024)


def cost(flops, moved):
    return pl.CostEstimate(flops=flops, bytes_accessed=moved, transcendentals=0)


def exp(x):
    return jnp.exp2(x * LOG2E)


def blocks(n):
    return [(c, min(c + BLOCK, n)) for c in range(0, n, BLOCK)]


def tiles(x):
    return [x[:, c : c + 128] for c in range(0, x.shape[1], 128)]


def own_kernel(mine, weight, target, acc, probs, stat):
    vocab = target.shape[1]
    for c, e in blocks(vocab):
        acc[:, c:e] = dot(mine[...], weight[:, c:e], 1, 0)
    wide = target[...].astype(F32)
    peak = jnp.max(wide, axis=1, keepdims=True)
    terms = exp(wide - peak)
    total = jnp.sum(terms, axis=1, keepdims=True)
    terms = terms / total
    probs[...] = terms
    mean = jnp.sum(terms * wide, axis=1, keepdims=True)
    lane = lax.broadcasted_iota(jnp.int32, stat.shape, 1)
    stat[...] = jnp.where(lane == 0, peak + jnp.log(total), mean)


def own_part(mine, weight, target):
    tokens, half = mine.shape
    vocab = target.shape[1]
    return pl.pallas_call(
        own_kernel,
        in_specs=[VMEM] * 3,
        out_specs=[VMEM] * 3,
        out_shape=[
            jax.ShapeDtypeStruct((tokens, vocab), F32),
            jax.ShapeDtypeStruct((tokens, vocab), F32),
            jax.ShapeDtypeStruct((tokens, 128), F32),
        ],
        compiler_params=params(24),
        cost_estimate=cost(2 * tokens * half * vocab, 2 * half * vocab),
        name="own_part",
    )(mine, weight, target)


def draft_kernel(theirs, acc, probs, stat, weight, draft, out, buffer, sems):
    tokens, vocab = draft.shape
    copies = []
    for j, (c, e) in enumerate(blocks(vocab)):
        part = pl.ds(c, e - c)
        copies.append(pltpu.make_async_copy(weight.at[:, part], buffer.at[:, part], sems.at[j]))
        copies[-1].start()
    peak = jnp.full((tokens, 128), -jnp.inf, F32)
    cross = jnp.zeros((tokens, 128), F32)
    for j, (c, e) in enumerate(blocks(vocab)):
        copies[j].wait()
        value = acc[:, c:e] + dot(theirs[...], buffer[:, c:e], 1, 0)
        draft[:, c:e] = value
        for tile, weighed in zip(tiles(value), tiles(probs[:, c:e] * value)):
            peak = jnp.maximum(peak, tile)
            cross = cross + weighed
    top = jnp.max(peak, axis=1, keepdims=True)
    total = jnp.zeros((tokens, 128), F32)
    for tile in tiles(draft[...]):
        total = total + exp(tile - top)
    lse_q = top + jnp.log(jnp.sum(total, axis=1, keepdims=True))
    mean = stat[:, 1:2] - jnp.sum(cross, axis=1, keepdims=True)
    lane = lax.broadcasted_iota(jnp.int32, stat.shape, 1)
    rows = jnp.where(lane == 0, stat[:, :1], jnp.where(lane == 1, mean, lse_q)).T
    for i in range(3):
        out[:, i * tokens : (i + 1) * tokens] = rows[i : i + 1]


def draft_part(theirs, acc, probs, stat, weight):
    tokens, half = theirs.shape
    vocab = acc.shape[1]
    return pl.pallas_call(
        draft_kernel,
        in_specs=[VMEM] * 4 + [HBM],
        out_specs=[VMEM] * 2,
        out_shape=[
            jax.ShapeDtypeStruct((tokens, vocab), F32),
            jax.ShapeDtypeStruct((1, 3 * tokens), F32),
        ],
        scratch_shapes=[pltpu.VMEM((half, vocab), BF16), pltpu.SemaphoreType.DMA((len(blocks(vocab)),))],
        compiler_params=params(24),
        cost_estimate=cost(2 * tokens * half * vocab, 2 * half * vocab),
        name="draft_part",
    )(theirs, acc, probs, stat, weight)


def back_kernel(factor, row, parts, draft, target, weight, weight_o, divergence, dlogits, out, stage, sems):
    half = weight.shape[0]
    per = half // COLS_PIECE
    tokens = draft.shape[0]
    each_t, mean, each_q = (parts[:, :, i * tokens : (i + 1) * tokens] for i in range(3))
    top_t, top_q = jnp.max(each_t, axis=0), jnp.max(each_q, axis=0)
    scale_t = exp(each_t - top_t)
    sum_t = jnp.sum(scale_t, axis=0)
    sum_q = jnp.sum(exp(each_q - top_q), axis=0)
    lse_t, lse_q = top_t + jnp.log(sum_t), top_q + jnp.log(sum_q)
    divergence[...] = jnp.sum(scale_t * mean, axis=0) / sum_t - lse_t + lse_q
    line = lax.broadcasted_iota(jnp.int32, (128, tokens), 0)
    turned = jnp.where(line == 0, lse_t, lse_q).T
    lse_t, lse_q = turned[:, :1], turned[:, 1:2]

    for c, e in blocks(draft.shape[1]):
        probs_q = exp(draft[:, c:e] - lse_q)
        probs_t = exp(target[:, c:e].astype(F32) - lse_t)
        dlogits[:, c:e] = ((probs_q - probs_t) * factor).astype(BF16)

    copies = []
    for j in range(2 * per):
        source = (weight, weight_o)[j // per]
        rows = source[j % per * COLS_PIECE : (j % per + 1) * COLS_PIECE]
        block = dot(dlogits[...], rows, 1, 1).astype(BF16)
        stage[j] = block.reshape(tokens // TOKENS_PIECE, TOKENS_PIECE, COLS_PIECE)
        place = lax.rem(row[0] * per + j, 2 * per)
        copies.append(pltpu.make_async_copy(stage.at[j], out.at[:, place], sems.at[j]))
        copies[-1].start()
    for copy in copies:
        copy.wait()


def back_part(factor, row, parts, draft, target, weight, weight_o):
    tokens, vocab = draft.shape
    half = weight.shape[0]
    down, across = tokens // TOKENS_PIECE, 2 * half // COLS_PIECE
    return pl.pallas_call(
        functools.partial(back_kernel, factor),
        in_specs=[pl.BlockSpec(memory_space=pltpu.SMEM)] + [VMEM] * 5,
        out_specs=[VMEM, VMEM, HBM],
        out_shape=[
            jax.ShapeDtypeStruct((1, tokens), F32),
            jax.ShapeDtypeStruct((tokens, vocab), BF16),
            jax.ShapeDtypeStruct((down, across, TOKENS_PIECE, COLS_PIECE), BF16),
        ],
        scratch_shapes=[
            pltpu.VMEM((across, down, TOKENS_PIECE, COLS_PIECE), BF16),
            pltpu.SemaphoreType.DMA((across,)),
        ],
        compiler_params=params(24),
        cost_estimate=cost(4 * tokens * half * vocab, 4 * half * vocab),
        name="back_part",
    )(row, parts, draft, target, weight, weight_o)


def sum_kernel(terms, out):
    total = terms[0].astype(F32)
    for i in range(1, terms.shape[0]):
        total = total + terms[i].astype(F32)
    out[...] = jnp.broadcast_to(total.astype(BF16)[None], out.shape)


def sum_part(terms):
    return pl.pallas_call(
        sum_kernel,
        in_specs=[VMEM],
        out_specs=VMEM,
        out_shape=jax.ShapeDtypeStruct(terms.shape, BF16),
        compiler_params=params(8),
        name="sum_part",
    )(terms)


def join_kernel(pieces, out, stage, sems):
    tokens, width = out.shape
    across = width // COLS_PIECE
    steps = sems.shape[0]
    copies = []
    for step in range(steps):
        rows = pl.ds(step * tokens // steps, tokens // steps)
        for i in range(step * pieces.shape[0] // steps, (step + 1) * pieces.shape[0] // steps):
            down = pl.ds(i // across * TOKENS_PIECE, TOKENS_PIECE)
            stage[down, pl.ds(i % across * COLS_PIECE, COLS_PIECE)] = pieces[i].astype(F32)
        copies.append(pltpu.make_async_copy(stage.at[rows], out.at[rows], sems.at[step]))
        copies[-1].start()
    for copy in copies:
        copy.wait()


def join_part(pieces, tokens, width):
    return pl.pallas_call(
        join_kernel,
        in_specs=[VMEM],
        out_specs=HBM,
        out_shape=jax.ShapeDtypeStruct((tokens, width), F32),
        scratch_shapes=[pltpu.VMEM((tokens, width), F32), pltpu.SemaphoreType.DMA((4,))],
        compiler_params=params(8),
        name="join_part",
    )(pieces)


def head_kernel(mine, mine_o, dlogits, dlogits_o, out):
    out[...] = dot(mine[...], dlogits[...], 0, 0) + dot(mine_o[...], dlogits_o[...], 0, 0)


def head_part(mine, mine_o, dlogits, dlogits_o):
    tokens, half = mine.shape
    vocab = dlogits.shape[1]
    step = 128
    column = pl.BlockSpec((tokens, step), lambda j: (0, j))
    return pl.pallas_call(
        head_kernel,
        grid=(half // step,),
        in_specs=[column, column, VMEM, VMEM],
        out_specs=pl.BlockSpec((step, vocab), lambda j: (j, 0)),
        out_shape=jax.ShapeDtypeStruct((half, vocab), F32),
        compiler_params=params(16),
        cost_estimate=cost(4 * tokens * half * vocab, 4 * half * vocab),
        name="head_part",
    )(mine, mine_o, dlogits, dlogits_o)


def shards(hidden, weight, target):
    n = lax.axis_size("vocab")
    row = lax.axis_index("rows")
    tokens, width = hidden.shape
    half, vocab = weight.shape

    with jax.named_scope("swap_weight"):
        weight_o = swap(weight)
    mine = lax.dynamic_slice_in_dim(hidden, row * half, half, 1)
    theirs = lax.dynamic_slice_in_dim(hidden, (1 - row) * half, half, 1)
    with jax.named_scope("swap_hidden"):
        mine_o = swap(theirs)

    acc, probs, stat = own_part(mine, weight, target)
    draft, part = draft_part(theirs, acc, probs, stat, weight_o)
    with jax.named_scope("share_stats"):
        parts = lax.all_to_all(jnp.broadcast_to(part[None], (n,) + part.shape), "vocab", 0, 0)
    divergence, dlogits, pieces = back_part(
        vocab * n / 1024.0, jnp.full((1,), row, jnp.int32), parts, draft, target, weight, weight_o
    )
    with jax.named_scope("swap_dlogits"):
        dlogits_o = swap(dlogits)
    with jax.named_scope("scatter_sum"):
        terms = lax.all_to_all(pieces.reshape(n, TOKENS_PIECE, COLS_PIECE), "vocab", 0, 0)
    totals = sum_part(terms)
    with jax.named_scope("gather"):
        gathered = lax.all_to_all(totals, "vocab", 0, 0)
    hidden_grad = join_part(gathered, tokens, width)
    head_grad = head_part(mine, mine_o, dlogits, dlogits_o)
    return (divergence.reshape(tokens), hidden_grad, head_grad)


def solution(mesh):
    return jax.shard_map(
        shards,
        mesh=mesh,
        in_specs=(P("rows", None), P("rows", "vocab"), P("rows", "vocab")),
        out_specs=(P("rows"), P("rows", None), P("rows", "vocab")),
        check_vma=False,
    )
```

```python
import functools
import math
import jax
import jax.numpy as jnp
from jax import lax
from jax.experimental import pallas as pl
from jax.experimental.pallas import tpu as pltpu
from jax.sharding import PartitionSpec as P

SWAP = ((0, 1), (1, 0))
TOKENS_PIECE = 16
COLS_PIECE = 512
BLOCK = 640
AHEAD = 2
LOG2E = math.log2(math.e)
F32, BF16 = jnp.float32, jnp.bfloat16
VMEM = pl.BlockSpec(memory_space=pltpu.VMEM)
HBM = pl.BlockSpec(memory_space=pltpu.HBM)
ANY = pl.BlockSpec(memory_space=pl.ANY)


def dot(a, b, ca, cb):
    return lax.dot_general(a, b, (((ca,), (cb,)), ((), ())), preferred_element_type=F32)


def swap(x):
    return lax.ppermute(x, "rows", SWAP)


def params(mib):
    return pltpu.CompilerParams(vmem_limit_bytes=mib * 1024 * 1024)


def cost(flops, moved):
    return pl.CostEstimate(flops=flops, bytes_accessed=moved, transcendentals=0)


def exp(x):
    return jnp.exp2(x * LOG2E)


def blocks(n):
    return [(c, min(c + BLOCK, n)) for c in range(0, n, BLOCK)]


def tiles(x):
    return [x[:, c : c + 128] for c in range(0, x.shape[1], 128)]


def own_kernel(mine, weight, target, acc, probs, stat):
    vocab = target.shape[1]
    for c, e in blocks(vocab):
        acc[:, c:e] = dot(mine[...], weight[:, c:e], 1, 0)
    wide = target[...].astype(F32)
    peak = jnp.max(wide, axis=1, keepdims=True)
    terms = exp(wide - peak)
    total = jnp.sum(terms, axis=1, keepdims=True)
    terms = terms / total
    probs[...] = terms
    mean = jnp.sum(terms * wide, axis=1, keepdims=True)
    lane = lax.broadcasted_iota(jnp.int32, stat.shape, 1)
    stat[...] = jnp.where(lane == 0, peak + jnp.log(total), mean)


def own_part(mine, weight, target):
    tokens, half = mine.shape
    vocab = target.shape[1]
    return pl.pallas_call(
        own_kernel,
        in_specs=[VMEM] * 3,
        out_specs=[VMEM] * 3,
        out_shape=[
            jax.ShapeDtypeStruct((tokens, vocab), F32),
            jax.ShapeDtypeStruct((tokens, vocab), F32),
            jax.ShapeDtypeStruct((tokens, 128), F32),
        ],
        compiler_params=params(24),
        cost_estimate=cost(2 * tokens * half * vocab, 2 * half * vocab),
        name="own_part",
    )(mine, weight, target)


def draft_kernel(theirs, acc, probs, stat, weight, draft, out, buffer, stage, sems, out_sems):
    tokens, vocab = stage.shape
    copies, results = [], []
    for j, (c, e) in enumerate(blocks(vocab)):
        part = pl.ds(c, e - c)
        copies.append(pltpu.make_async_copy(weight.at[:, part], buffer.at[:, part], sems.at[j]))
    for copy in copies[:AHEAD]:
        copy.start()
    peak = jnp.full((tokens, 128), -jnp.inf, F32)
    cross = jnp.zeros((tokens, 128), F32)
    for j, (c, e) in enumerate(blocks(vocab)):
        copies[j].wait()
        for copy in copies[j + AHEAD : j + AHEAD + 1]:
            copy.start()
        value = acc[:, c:e] + dot(theirs[...], buffer[:, c:e], 1, 0)
        stage[:, c:e] = value
        part = pl.ds(c, e - c)
        results.append(pltpu.make_async_copy(stage.at[:, part], draft.at[:, part], out_sems.at[j]))
        results[-1].start()
        for tile, weighed in zip(tiles(value), tiles(probs[:, c:e] * value)):
            peak = jnp.maximum(peak, tile)
            cross = cross + weighed
    top = jnp.max(peak, axis=1, keepdims=True)
    total = jnp.zeros((tokens, 128), F32)
    for tile in tiles(stage[...]):
        total = total + exp(tile - top)
    lse_q = top + jnp.log(jnp.sum(total, axis=1, keepdims=True))
    mean = stat[:, 1:2] - jnp.sum(cross, axis=1, keepdims=True)
    lane = lax.broadcasted_iota(jnp.int32, stat.shape, 1)
    rows = jnp.where(lane == 0, stat[:, :1], jnp.where(lane == 1, mean, lse_q)).T
    for i in range(3):
        out[:, i * tokens : (i + 1) * tokens] = rows[i : i + 1]
    for result in results:
        result.wait()


def draft_part(theirs, acc, probs, stat, weight):
    tokens, half = theirs.shape
    vocab = acc.shape[1]
    steps = len(blocks(vocab))
    return pl.pallas_call(
        draft_kernel,
        in_specs=[VMEM] * 4 + [ANY],
        out_specs=[ANY, VMEM],
        out_shape=[
            jax.ShapeDtypeStruct((tokens, vocab), F32),
            jax.ShapeDtypeStruct((1, 3 * tokens), F32),
        ],
        scratch_shapes=[
            pltpu.VMEM((half, vocab), BF16),
            pltpu.VMEM((tokens, vocab), F32),
            pltpu.SemaphoreType.DMA((steps,)),
            pltpu.SemaphoreType.DMA((steps,)),
        ],
        compiler_params=params(20),
        cost_estimate=cost(2 * tokens * half * vocab, 2 * half * vocab),
        name="draft_part",
    )(theirs, acc, probs, stat, weight)


def back_kernel(
    factor, row, parts, draft, target, weight, weight_o, divergence, dlogits, out, buffer, stage, sems, out_sems
):
    half = weight.shape[0]
    per = half // COLS_PIECE
    tokens = draft.shape[0]
    down = tokens // TOKENS_PIECE
    loads, copies = [], []
    for j in range(2 * per):
        source = (weight, weight_o)[j // per].at[pl.ds(j % per * COLS_PIECE, COLS_PIECE)]
        loads.append(pltpu.make_async_copy(source, buffer.at[j], sems.at[j]))
    for load in loads[:AHEAD]:
        load.start()

    each_t, mean, each_q = (parts[:, :, i * tokens : (i + 1) * tokens] for i in range(3))
    top_t, top_q = jnp.max(each_t, axis=0), jnp.max(each_q, axis=0)
    scale_t = exp(each_t - top_t)
    sum_t = jnp.sum(scale_t, axis=0)
    sum_q = jnp.sum(exp(each_q - top_q), axis=0)
    lse_t, lse_q = top_t + jnp.log(sum_t), top_q + jnp.log(sum_q)
    divergence[...] = jnp.sum(scale_t * mean, axis=0) / sum_t - lse_t + lse_q
    line = lax.broadcasted_iota(jnp.int32, (128, tokens), 0)
    turned = jnp.where(line == 0, lse_t, lse_q).T
    lse_t, lse_q = turned[:, :1], turned[:, 1:2]

    for c, e in blocks(draft.shape[1]):
        probs_q = exp(draft[:, c:e] - lse_q)
        probs_t = exp(target[:, c:e].astype(F32) - lse_t)
        dlogits[:, c:e] = ((probs_q - probs_t) * factor).astype(BF16)

    for j in range(2 * per):
        loads[j].wait()
        for load in loads[j + AHEAD : j + AHEAD + 1]:
            load.start()
        block = dot(dlogits[...], buffer[j], 1, 1).astype(BF16)
        stage[j] = block.reshape(down, TOKENS_PIECE, COLS_PIECE)
        place = lax.rem(row[0] * per + j, 2 * per)
        copies.append(pltpu.make_async_copy(stage.at[j], out.at[pl.ds(place * down, down)], out_sems.at[j]))
        copies[-1].start()
    for copy in copies:
        copy.wait()


def back_part(factor, row, parts, draft, target, weight, weight_o):
    tokens, vocab = draft.shape
    half = weight.shape[0]
    down, across = tokens // TOKENS_PIECE, 2 * half // COLS_PIECE
    return pl.pallas_call(
        functools.partial(back_kernel, factor),
        in_specs=[pl.BlockSpec(memory_space=pltpu.SMEM)] + [VMEM] * 3 + [ANY] * 2,
        out_specs=[VMEM, VMEM, ANY],
        out_shape=[
            jax.ShapeDtypeStruct((1, tokens), F32),
            jax.ShapeDtypeStruct((tokens, vocab), BF16),
            jax.ShapeDtypeStruct((down * across, TOKENS_PIECE, COLS_PIECE), BF16),
        ],
        scratch_shapes=[
            pltpu.VMEM((across, COLS_PIECE, vocab), BF16),
            pltpu.VMEM((across, down, TOKENS_PIECE, COLS_PIECE), BF16),
            pltpu.SemaphoreType.DMA((across,)),
            pltpu.SemaphoreType.DMA((across,)),
        ],
        compiler_params=params(24),
        cost_estimate=cost(4 * tokens * half * vocab, 4 * half * vocab),
        name="back_part",
    )(row, parts, draft, target, weight, weight_o)


def sum_kernel(terms, out):
    total = terms[0].astype(F32)
    for i in range(1, terms.shape[0]):
        total = total + terms[i].astype(F32)
    out[...] = jnp.broadcast_to(total.astype(BF16)[None], out.shape)


def sum_part(terms):
    return pl.pallas_call(
        sum_kernel,
        in_specs=[VMEM],
        out_specs=VMEM,
        out_shape=jax.ShapeDtypeStruct(terms.shape, BF16),
        compiler_params=params(8),
        name="sum_part",
    )(terms)


def join_kernel(pieces, out, stage, sems):
    tokens, width = out.shape
    down = tokens // TOKENS_PIECE
    steps = sems.shape[0]
    copies = []
    for step in range(steps):
        rows = pl.ds(step * tokens // steps, tokens // steps)
        for i in range(step * down // steps, (step + 1) * down // steps):
            for j in range(width // COLS_PIECE):
                place = pl.ds(i * TOKENS_PIECE, TOKENS_PIECE), pl.ds(j * COLS_PIECE, COLS_PIECE)
                stage[place] = pieces[j * down + i].astype(F32)
        copies.append(pltpu.make_async_copy(stage.at[rows], out.at[rows], sems.at[step]))
        copies[-1].start()
    for copy in copies:
        copy.wait()


def join_part(pieces, tokens, width):
    return pl.pallas_call(
        join_kernel,
        in_specs=[VMEM],
        out_specs=HBM,
        out_shape=jax.ShapeDtypeStruct((tokens, width), F32),
        scratch_shapes=[pltpu.VMEM((tokens, width), F32), pltpu.SemaphoreType.DMA((4,))],
        compiler_params=params(8),
        name="join_part",
    )(pieces)


def head_kernel(mine, mine_o, dlogits, dlogits_o, out):
    out[...] = dot(mine[...], dlogits[...], 0, 0) + dot(mine_o[...], dlogits_o[...], 0, 0)


def head_part(mine, mine_o, dlogits, dlogits_o):
    tokens, half = mine.shape
    vocab = dlogits.shape[1]
    step = 128
    column = pl.BlockSpec((tokens, step), lambda j: (0, j))
    return pl.pallas_call(
        head_kernel,
        grid=(half // step,),
        in_specs=[column, column, VMEM, VMEM],
        out_specs=pl.BlockSpec((step, vocab), lambda j: (j, 0)),
        out_shape=jax.ShapeDtypeStruct((half, vocab), F32),
        compiler_params=params(16),
        cost_estimate=cost(4 * tokens * half * vocab, 4 * half * vocab),
        name="head_part",
    )(mine, mine_o, dlogits, dlogits_o)


def shards(hidden, weight, target):
    n = lax.axis_size("vocab")
    row = lax.axis_index("rows")
    tokens, width = hidden.shape
    half, vocab = weight.shape

    with jax.named_scope("swap_weight"):
        weight_o = swap(weight)
    mine = lax.dynamic_slice_in_dim(hidden, row * half, half, 1)
    theirs = lax.dynamic_slice_in_dim(hidden, (1 - row) * half, half, 1)
    with jax.named_scope("swap_hidden"):
        mine_o = swap(theirs)

    acc, probs, stat = own_part(mine, weight, target)
    draft, part = draft_part(theirs, acc, probs, stat, weight_o)
    with jax.named_scope("share_stats"):
        parts = lax.all_to_all(jnp.broadcast_to(part[None], (n,) + part.shape), "vocab", 0, 0)
    divergence, dlogits, pieces = back_part(
        vocab * n / 1024.0, jnp.full((1,), row, jnp.int32), parts, draft, target, weight, weight_o
    )
    with jax.named_scope("swap_dlogits"):
        dlogits_o = swap(dlogits)
    with jax.named_scope("scatter_sum"):
        terms = lax.all_to_all(pieces, "vocab", 0, 0)
    totals = sum_part(terms)
    with jax.named_scope("gather"):
        gathered = lax.all_to_all(totals, "vocab", 0, 0)
    hidden_grad = join_part(gathered, tokens, width)
    head_grad = head_part(mine, mine_o, dlogits, dlogits_o)
    return (divergence.reshape(tokens), hidden_grad, head_grad)


def solution(mesh):
    return jax.shard_map(
        shards,
        mesh=mesh,
        in_specs=(P("rows", None), P("rows", "vocab"), P("rows", "vocab")),
        out_specs=(P("rows"), P("rows", None), P("rows", "vocab")),
        check_vma=False,
    )
```

```python
import functools
import math
import jax
import jax.numpy as jnp
from jax import lax
from jax.experimental import pallas as pl
from jax.experimental.pallas import tpu as pltpu
from jax.sharding import PartitionSpec as P

SWAP = ((0, 1), (1, 0))
TOKENS_PIECE = 16
COLS_PIECE = 512
BLOCK = 640
AHEAD = 2
LOG2E = math.log2(math.e)
F32, BF16 = jnp.float32, jnp.bfloat16
VMEM = pl.BlockSpec(memory_space=pltpu.VMEM)
HBM = pl.BlockSpec(memory_space=pltpu.HBM)
ANY = pl.BlockSpec(memory_space=pl.ANY)


def dot(a, b, ca, cb):
    return lax.dot_general(a, b, (((ca,), (cb,)), ((), ())), preferred_element_type=F32)


def swap(x):
    return lax.ppermute(x, "rows", SWAP)


def params(mib):
    return pltpu.CompilerParams(vmem_limit_bytes=mib * 1024 * 1024)


def cost(flops, moved):
    return pl.CostEstimate(flops=flops, bytes_accessed=moved, transcendentals=0)


def exp(x):
    return jnp.exp2(x * LOG2E)


def blocks(n):
    return [(c, min(c + BLOCK, n)) for c in range(0, n, BLOCK)]


def tiles(x):
    return [x[:, c : c + 128] for c in range(0, x.shape[1], 128)]


def stat_rows(tokens):
    return pl.cdiv(3 * tokens // 128, 8) * 8


def own_kernel(mine, weight, target, acc, probs, stat):
    vocab = target.shape[1]
    for c, e in blocks(vocab):
        acc[:, c:e] = dot(mine[...], weight[:, c:e], 1, 0)
    wide = target[...].astype(F32)
    peak = jnp.max(wide, axis=1, keepdims=True)
    terms = exp(wide - peak)
    total = jnp.sum(terms, axis=1, keepdims=True)
    terms = terms / total
    probs[...] = terms
    mean = jnp.sum(terms * wide, axis=1, keepdims=True)
    lane = lax.broadcasted_iota(jnp.int32, stat.shape, 1)
    stat[...] = jnp.where(lane == 0, peak + jnp.log(total), mean)


def own_part(mine, weight, target):
    tokens, half = mine.shape
    vocab = target.shape[1]
    return pl.pallas_call(
        own_kernel,
        in_specs=[VMEM] * 3,
        out_specs=[VMEM] * 3,
        out_shape=[
            jax.ShapeDtypeStruct((tokens, vocab), F32),
            jax.ShapeDtypeStruct((tokens, vocab), F32),
            jax.ShapeDtypeStruct((tokens, 128), F32),
        ],
        compiler_params=params(24),
        cost_estimate=cost(2 * tokens * half * vocab, 2 * half * vocab),
        name="own_part",
    )(mine, weight, target)


def draft_kernel(theirs, acc, probs, stat, weight, draft, out, buffer, sems):
    tokens, vocab = draft.shape
    copies = []
    for j, (c, e) in enumerate(blocks(vocab)):
        part = pl.ds(c, e - c)
        copies.append(pltpu.make_async_copy(weight.at[:, part], buffer.at[:, part], sems.at[j]))
    for copy in copies[:AHEAD]:
        copy.start()
    peak = jnp.full((tokens, 128), -jnp.inf, F32)
    cross = jnp.zeros((tokens, 128), F32)
    for j, (c, e) in enumerate(blocks(vocab)):
        copies[j].wait()
        for copy in copies[j + AHEAD : j + AHEAD + 1]:
            copy.start()
        value = acc[:, c:e] + dot(theirs[...], buffer[:, c:e], 1, 0)
        draft[:, c:e] = value
        for tile, weighed in zip(tiles(value), tiles(probs[:, c:e] * value)):
            peak = jnp.maximum(peak, tile)
            cross = cross + weighed
    top = jnp.max(peak, axis=1, keepdims=True)
    total = jnp.zeros((tokens, 128), F32)
    for tile in tiles(draft[...]):
        total = total + exp(tile - top)
    lse_q = top + jnp.log(jnp.sum(total, axis=1, keepdims=True))
    mean = stat[:, 1:2] - jnp.sum(cross, axis=1, keepdims=True)
    lane = lax.broadcasted_iota(jnp.int32, stat.shape, 1)
    rows = jnp.where(lane == 0, stat[:, :1], jnp.where(lane == 1, mean, lse_q)).T
    out[...] = jnp.zeros(out.shape, F32)
    for i in range(3):
        for k in range(tokens // 128):
            at = i * (tokens // 128) + k
            out[at : at + 1] = rows[i : i + 1, k * 128 : (k + 1) * 128]


def draft_part(theirs, acc, probs, stat, weight):
    tokens, half = theirs.shape
    vocab = acc.shape[1]
    steps = len(blocks(vocab))
    return pl.pallas_call(
        draft_kernel,
        in_specs=[VMEM] * 4 + [ANY],
        out_specs=[VMEM] * 3,
        out_shape=[
            jax.ShapeDtypeStruct((tokens, vocab), F32),
            jax.ShapeDtypeStruct((stat_rows(tokens), 128), F32),
            jax.ShapeDtypeStruct((half, vocab), BF16),
        ],
        scratch_shapes=[pltpu.SemaphoreType.DMA((steps,))],
        compiler_params=params(20),
        cost_estimate=cost(2 * tokens * half * vocab, 2 * half * vocab),
        name="draft_part",
    )(theirs, acc, probs, stat, weight)


def logits_kernel(factor, parts, draft, target, divergence, dlogits):
    lines = draft.shape[0] // 128
    every = parts[...]
    top = jnp.max(every, axis=0)
    scale = exp(every - top)
    lse = top + jnp.log(jnp.sum(scale, axis=0))
    cross = jnp.sum(scale[:, :lines] * every[:, lines : 2 * lines], axis=0)
    mean = cross / jnp.sum(scale[:, :lines], axis=0)
    result = mean - lse[:lines] + lse[2 * lines : 3 * lines]
    for k in range(lines):
        divergence[:, k * 128 : (k + 1) * 128] = result[k : k + 1]
    turned = jnp.concatenate([lse, jnp.zeros((128 - lse.shape[0], 128), F32)], axis=0).T
    lse_t = jnp.concatenate([turned[:, k : k + 1] for k in range(lines)], axis=0)
    lse_q = jnp.concatenate([turned[:, 2 * lines + k : 2 * lines + k + 1] for k in range(lines)], axis=0)
    for c, e in blocks(draft.shape[1]):
        probs_q = exp(draft[:, c:e] - lse_q)
        probs_t = exp(target[:, c:e].astype(F32) - lse_t)
        dlogits[:, c:e] = ((probs_q - probs_t) * factor).astype(BF16)


def logits_part(factor, parts, draft, target):
    tokens, vocab = draft.shape
    return pl.pallas_call(
        functools.partial(logits_kernel, factor),
        in_specs=[VMEM] * 3,
        out_specs=[VMEM] * 2,
        out_shape=[
            jax.ShapeDtypeStruct((1, tokens), F32),
            jax.ShapeDtypeStruct((tokens, vocab), BF16),
        ],
        compiler_params=params(16),
        cost_estimate=cost(8 * tokens * vocab, 8 * tokens * vocab),
        name="logits_part",
    )(parts, draft, target)


def back_kernel(row, dlogits, weight, weight_o, out):
    half = weight.shape[0]
    per = half // COLS_PIECE
    down = dlogits.shape[0] // TOKENS_PIECE
    for j in range(2 * per):
        rows = pl.ds(j % per * COLS_PIECE, COLS_PIECE)
        block = dot(dlogits[...], (weight, weight_o)[j // per][rows], 1, 1).astype(BF16)
        place = lax.rem(row[0] * per + j, 2 * per)
        out[pl.ds(place * down, down)] = block.reshape(down, TOKENS_PIECE, COLS_PIECE)


def back_part(row, dlogits, weight, weight_o):
    tokens, vocab = dlogits.shape
    half = weight.shape[0]
    pieces = (tokens // TOKENS_PIECE) * (2 * half // COLS_PIECE)
    return pl.pallas_call(
        back_kernel,
        in_specs=[pl.BlockSpec(memory_space=pltpu.SMEM)] + [VMEM] * 3,
        out_specs=VMEM,
        out_shape=jax.ShapeDtypeStruct((pieces, TOKENS_PIECE, COLS_PIECE), BF16),
        compiler_params=params(16),
        cost_estimate=cost(4 * tokens * half * vocab, 4 * half * vocab),
        name="back_part",
    )(row, dlogits, weight, weight_o)


def sum_kernel(terms, out):
    total = terms[0].astype(F32)
    for i in range(1, terms.shape[0]):
        total = total + terms[i].astype(F32)
    out[...] = jnp.broadcast_to(total.astype(BF16)[None], out.shape)


def sum_part(terms):
    return pl.pallas_call(
        sum_kernel,
        in_specs=[VMEM],
        out_specs=VMEM,
        out_shape=jax.ShapeDtypeStruct(terms.shape, BF16),
        compiler_params=params(8),
        name="sum_part",
    )(terms)


def join_kernel(pieces, out, stage, sems):
    tokens, width = out.shape
    down = tokens // TOKENS_PIECE
    steps = sems.shape[0]
    copies = []
    for step in range(steps):
        rows = pl.ds(step * tokens // steps, tokens // steps)
        for i in range(step * down // steps, (step + 1) * down // steps):
            for j in range(width // COLS_PIECE):
                place = pl.ds(i * TOKENS_PIECE, TOKENS_PIECE), pl.ds(j * COLS_PIECE, COLS_PIECE)
                stage[place] = pieces[j * down + i].astype(F32)
        copies.append(pltpu.make_async_copy(stage.at[rows], out.at[rows], sems.at[step]))
        copies[-1].start()
    for copy in copies:
        copy.wait()


def join_part(pieces, tokens, width):
    return pl.pallas_call(
        join_kernel,
        in_specs=[VMEM],
        out_specs=HBM,
        out_shape=jax.ShapeDtypeStruct((tokens, width), F32),
        scratch_shapes=[pltpu.VMEM((tokens, width), F32), pltpu.SemaphoreType.DMA((4,))],
        compiler_params=params(8),
        name="join_part",
    )(pieces)


def head_kernel(mine, mine_o, dlogits, dlogits_o, out):
    out[...] = dot(mine[...], dlogits[...], 0, 0) + dot(mine_o[...], dlogits_o[...], 0, 0)


def head_part(mine, mine_o, dlogits, dlogits_o):
    tokens, half = mine.shape
    vocab = dlogits.shape[1]
    step = 128
    column = pl.BlockSpec((tokens, step), lambda j: (0, j))
    return pl.pallas_call(
        head_kernel,
        grid=(half // step,),
        in_specs=[column, column, VMEM, VMEM],
        out_specs=pl.BlockSpec((step, vocab), lambda j: (j, 0)),
        out_shape=jax.ShapeDtypeStruct((half, vocab), F32),
        compiler_params=params(16),
        cost_estimate=cost(4 * tokens * half * vocab, 4 * half * vocab),
        name="head_part",
    )(mine, mine_o, dlogits, dlogits_o)


def shards(hidden, weight, target):
    n = lax.axis_size("vocab")
    row = lax.axis_index("rows")
    tokens, width = hidden.shape
    half, vocab = weight.shape

    with jax.named_scope("swap_weight"):
        weight_o = swap(weight)
    mine = lax.dynamic_slice_in_dim(hidden, row * half, half, 1)
    theirs = lax.dynamic_slice_in_dim(hidden, (1 - row) * half, half, 1)
    with jax.named_scope("swap_hidden"):
        mine_o = swap(theirs)

    acc, probs, stat = own_part(mine, weight, target)
    draft, part, weight_o = draft_part(theirs, acc, probs, stat, weight_o)
    with jax.named_scope("share_stats"):
        parts = lax.all_to_all(jnp.broadcast_to(part[None], (n,) + part.shape), "vocab", 0, 0)
    divergence, dlogits = logits_part(vocab * n / 1024.0, parts, draft, target)
    with jax.named_scope("swap_dlogits"):
        dlogits_o = swap(dlogits)
    pieces = back_part(jnp.full((1,), row, jnp.int32), dlogits, weight, weight_o)
    with jax.named_scope("scatter_sum"):
        terms = lax.all_to_all(pieces, "vocab", 0, 0)
    totals = sum_part(terms)
    with jax.named_scope("gather"):
        gathered = lax.all_to_all(totals, "vocab", 0, 0)
    hidden_grad = join_part(gathered, tokens, width)
    head_grad = head_part(mine, mine_o, dlogits, dlogits_o)
    return (divergence.reshape(tokens), hidden_grad, head_grad)


def solution(mesh):
    return jax.shard_map(
        shards,
        mesh=mesh,
        in_specs=(P("rows", None), P("rows", "vocab"), P("rows", "vocab")),
        out_specs=(P("rows"), P("rows", None), P("rows", "vocab")),
        check_vma=False,
    )
```

```python
import functools
import math
import jax
import jax.numpy as jnp
from jax import lax
from jax.experimental import pallas as pl
from jax.experimental.pallas import tpu as pltpu
from jax.sharding import PartitionSpec as P

SWAP = ((0, 1), (1, 0))
TOKENS_PIECE = 16
COLS_PIECE = 512
BLOCK = 640
LOG2E = math.log2(math.e)
F32, BF16 = jnp.float32, jnp.bfloat16
VMEM = pl.BlockSpec(memory_space=pltpu.VMEM)
HBM = pl.BlockSpec(memory_space=pltpu.HBM)
ANY = pl.BlockSpec(memory_space=pl.ANY)


def dot(a, b, ca, cb):
    return lax.dot_general(a, b, (((ca,), (cb,)), ((), ())), preferred_element_type=F32)


def swap(x):
    return lax.ppermute(x, "rows", SWAP)


def params(mib):
    return pltpu.CompilerParams(vmem_limit_bytes=mib * 1024 * 1024)


def cost(flops, moved):
    return pl.CostEstimate(flops=flops, bytes_accessed=moved, transcendentals=0)


def exp(x):
    return jnp.exp2(x * LOG2E)


def blocks(n):
    return [(c, min(c + BLOCK, n)) for c in range(0, n, BLOCK)]


def tiles(x):
    return [x[:, c : c + 128] for c in range(0, x.shape[1], 128)]


def stat_rows(tokens):
    return pl.cdiv(3 * tokens // 128, 8) * 8


def load(source, target, sems):
    copies = []
    for j, (c, e) in enumerate(blocks(source.shape[1])):
        part = pl.ds(c, e - c)
        copies.append(pltpu.make_async_copy(source.at[:, part], target.at[:, part], sems.at[j]))
        copies[-1].start()
    return copies


def own_kernel(mine, target, weight, acc, probs, stat, buffer, sems):
    vocab = target.shape[1]
    copies = load(weight, buffer, sems)
    wide = target[...].astype(F32)
    peak = jnp.max(wide, axis=1, keepdims=True)
    terms = exp(wide - peak)
    total = jnp.sum(terms, axis=1, keepdims=True)
    terms = terms / total
    probs[...] = terms
    mean = jnp.sum(terms * wide, axis=1, keepdims=True)
    lane = lax.broadcasted_iota(jnp.int32, stat.shape, 1)
    stat[...] = jnp.where(lane == 0, peak + jnp.log(total), mean)
    for copy, (c, e) in zip(copies, blocks(vocab)):
        copy.wait()
        acc[:, c:e] = dot(mine[...], buffer[:, c:e], 1, 0)


def own_part(mine, target, weight):
    tokens, half = mine.shape
    vocab = target.shape[1]
    return pl.pallas_call(
        own_kernel,
        in_specs=[VMEM] * 2 + [ANY],
        out_specs=[VMEM] * 4,
        out_shape=[
            jax.ShapeDtypeStruct((tokens, vocab), F32),
            jax.ShapeDtypeStruct((tokens, vocab), F32),
            jax.ShapeDtypeStruct((tokens, 128), F32),
            jax.ShapeDtypeStruct((half, vocab), BF16),
        ],
        scratch_shapes=[pltpu.SemaphoreType.DMA((len(blocks(vocab)),))],
        compiler_params=params(16),
        cost_estimate=cost(2 * tokens * half * vocab, 2 * half * vocab),
        name="own_part",
    )(mine, target, weight)


def draft_kernel(theirs, acc, probs, stat, weight, draft, out, buffer, sems):
    tokens, vocab = draft.shape
    copies = load(weight, buffer, sems)
    peak = jnp.full((tokens, 128), -jnp.inf, F32)
    cross = jnp.zeros((tokens, 128), F32)
    for j, (c, e) in enumerate(blocks(vocab)):
        copies[j].wait()
        value = acc[:, c:e] + dot(theirs[...], buffer[:, c:e], 1, 0)
        draft[:, c:e] = value
        for tile, weighed in zip(tiles(value), tiles(probs[:, c:e] * value)):
            peak = jnp.maximum(peak, tile)
            cross = cross + weighed
    top = jnp.max(peak, axis=1, keepdims=True)
    total = jnp.zeros((tokens, 128), F32)
    for tile in tiles(draft[...]):
        total = total + exp(tile - top)
    lse_q = top + jnp.log(jnp.sum(total, axis=1, keepdims=True))
    mean = stat[:, 1:2] - jnp.sum(cross, axis=1, keepdims=True)
    lane = lax.broadcasted_iota(jnp.int32, stat.shape, 1)
    rows = jnp.where(lane == 0, stat[:, :1], jnp.where(lane == 1, mean, lse_q)).T
    out[...] = jnp.zeros(out.shape, F32)
    for i in range(3):
        for k in range(tokens // 128):
            at = i * (tokens // 128) + k
            out[at : at + 1] = rows[i : i + 1, k * 128 : (k + 1) * 128]


def draft_part(theirs, acc, probs, stat, weight):
    tokens, half = theirs.shape
    vocab = acc.shape[1]
    steps = len(blocks(vocab))
    return pl.pallas_call(
        draft_kernel,
        in_specs=[VMEM] * 4 + [ANY],
        out_specs=[VMEM] * 3,
        out_shape=[
            jax.ShapeDtypeStruct((tokens, vocab), F32),
            jax.ShapeDtypeStruct((stat_rows(tokens), 128), F32),
            jax.ShapeDtypeStruct((half, vocab), BF16),
        ],
        scratch_shapes=[pltpu.SemaphoreType.DMA((steps,))],
        compiler_params=params(20),
        cost_estimate=cost(2 * tokens * half * vocab, 2 * half * vocab),
        name="draft_part",
    )(theirs, acc, probs, stat, weight)


def back_kernel(factor, row, parts, draft, target, weight, weight_o, divergence, dlogits, out):
    lines = draft.shape[0] // 128
    every = parts[...]
    top = jnp.max(every, axis=0)
    scale = exp(every - top)
    lse = top + jnp.log(jnp.sum(scale, axis=0))
    cross = jnp.sum(scale[:, :lines] * every[:, lines : 2 * lines], axis=0)
    mean = cross / jnp.sum(scale[:, :lines], axis=0)
    result = mean - lse[:lines] + lse[2 * lines : 3 * lines]
    for k in range(lines):
        divergence[:, k * 128 : (k + 1) * 128] = result[k : k + 1]
    turned = jnp.concatenate([lse, jnp.zeros((128 - lse.shape[0], 128), F32)], axis=0).T
    lse_t = jnp.concatenate([turned[:, k : k + 1] for k in range(lines)], axis=0)
    lse_q = jnp.concatenate([turned[:, 2 * lines + k : 2 * lines + k + 1] for k in range(lines)], axis=0)

    half = weight.shape[0]
    per = half // COLS_PIECE
    down = dlogits.shape[0] // TOKENS_PIECE
    sums = [None] * (2 * per)
    for c, e in blocks(draft.shape[1]):
        probs_q = exp(draft[:, c:e] - lse_q)
        probs_t = exp(target[:, c:e].astype(F32) - lse_t)
        block = ((probs_q - probs_t) * factor).astype(BF16)
        dlogits[:, c:e] = block
        for j in range(2 * per):
            rows = pl.ds(j % per * COLS_PIECE, COLS_PIECE)
            term = dot(block, (weight, weight_o)[j // per][rows, c:e], 1, 1)
            sums[j] = term if sums[j] is None else sums[j] + term
    for j in range(2 * per):
        place = lax.rem(row[0] * per + j, 2 * per)
        out[pl.ds(place * down, down)] = sums[j].astype(BF16).reshape(down, TOKENS_PIECE, COLS_PIECE)


def back_part(factor, row, parts, draft, target, weight, weight_o):
    tokens, vocab = draft.shape
    half = weight.shape[0]
    pieces = (tokens // TOKENS_PIECE) * (2 * half // COLS_PIECE)
    return pl.pallas_call(
        functools.partial(back_kernel, factor),
        in_specs=[pl.BlockSpec(memory_space=pltpu.SMEM)] + [VMEM] * 5,
        out_specs=[VMEM] * 3,
        out_shape=[
            jax.ShapeDtypeStruct((1, tokens), F32),
            jax.ShapeDtypeStruct((tokens, vocab), BF16),
            jax.ShapeDtypeStruct((pieces, TOKENS_PIECE, COLS_PIECE), BF16),
        ],
        compiler_params=params(16),
        cost_estimate=cost(4 * tokens * half * vocab, 4 * half * vocab),
        name="back_part",
    )(row, parts, draft, target, weight, weight_o)


def sum_kernel(terms, out):
    total = terms[0].astype(F32)
    for i in range(1, terms.shape[0]):
        total = total + terms[i].astype(F32)
    out[...] = jnp.broadcast_to(total.astype(BF16)[None], out.shape)


def sum_part(terms):
    return pl.pallas_call(
        sum_kernel,
        in_specs=[VMEM],
        out_specs=VMEM,
        out_shape=jax.ShapeDtypeStruct(terms.shape, BF16),
        compiler_params=params(8),
        name="sum_part",
    )(terms)


def join_kernel(pieces, out, stage, sems):
    tokens, width = out.shape
    down = tokens // TOKENS_PIECE
    steps = sems.shape[0]
    copies = []
    for step in range(steps):
        rows = pl.ds(step * tokens // steps, tokens // steps)
        for i in range(step * down // steps, (step + 1) * down // steps):
            for j in range(width // COLS_PIECE):
                place = pl.ds(i * TOKENS_PIECE, TOKENS_PIECE), pl.ds(j * COLS_PIECE, COLS_PIECE)
                stage[place] = pieces[j * down + i].astype(F32)
        copies.append(pltpu.make_async_copy(stage.at[rows], out.at[rows], sems.at[step]))
        copies[-1].start()
    for copy in copies:
        copy.wait()


def join_part(pieces, tokens, width):
    return pl.pallas_call(
        join_kernel,
        in_specs=[VMEM],
        out_specs=HBM,
        out_shape=jax.ShapeDtypeStruct((tokens, width), F32),
        scratch_shapes=[pltpu.VMEM((tokens, width), F32), pltpu.SemaphoreType.DMA((4,))],
        compiler_params=params(8),
        name="join_part",
    )(pieces)


def head_kernel(mine, mine_o, dlogits, dlogits_o, out):
    out[...] = dot(mine[...], dlogits[...], 0, 0) + dot(mine_o[...], dlogits_o[...], 0, 0)


def head_part(mine, mine_o, dlogits, dlogits_o):
    tokens, half = mine.shape
    vocab = dlogits.shape[1]
    step = 128
    column = pl.BlockSpec((tokens, step), lambda j: (0, j))
    return pl.pallas_call(
        head_kernel,
        grid=(half // step,),
        in_specs=[column, column, VMEM, VMEM],
        out_specs=pl.BlockSpec((step, vocab), lambda j: (j, 0)),
        out_shape=jax.ShapeDtypeStruct((half, vocab), F32),
        compiler_params=params(16),
        cost_estimate=cost(4 * tokens * half * vocab, 4 * half * vocab),
        name="head_part",
    )(mine, mine_o, dlogits, dlogits_o)


def shards(hidden, weight, target):
    n = lax.axis_size("vocab")
    row = lax.axis_index("rows")
    tokens, width = hidden.shape
    half, vocab = weight.shape

    with jax.named_scope("swap_weight"):
        weight_o = swap(weight)
    mine = lax.dynamic_slice_in_dim(hidden, row * half, half, 1)
    theirs = lax.dynamic_slice_in_dim(hidden, (1 - row) * half, half, 1)

    acc, probs, stat, weight_v = own_part(mine, target, weight)
    draft, part, weight_o = draft_part(theirs, acc, probs, stat, weight_o)
    theirs, part = lax.optimization_barrier((theirs, part))
    with jax.named_scope("swap_hidden"):
        mine_o = swap(theirs)
    with jax.named_scope("share_stats"):
        parts = lax.all_to_all(jnp.broadcast_to(part[None], (n,) + part.shape), "vocab", 0, 0)
    divergence, dlogits, pieces = back_part(
        vocab * n / 1024.0, jnp.full((1,), row, jnp.int32), parts, draft, target, weight_v, weight_o
    )
    with jax.named_scope("scatter_sum"):
        terms = lax.all_to_all(pieces, "vocab", 0, 0)
    dlogits, terms = lax.optimization_barrier((dlogits, terms))
    with jax.named_scope("swap_dlogits"):
        dlogits_o = swap(dlogits)
    totals = sum_part(terms)
    with jax.named_scope("gather"):
        gathered = lax.all_to_all(totals, "vocab", 0, 0)
    head_grad = head_part(mine, mine_o, dlogits, dlogits_o)
    gathered, head_grad = lax.optimization_barrier((gathered, head_grad))
    hidden_grad = join_part(gathered, tokens, width)
    return (divergence.reshape(tokens), hidden_grad, head_grad)


def solution(mesh):
    return jax.shard_map(
        shards,
        mesh=mesh,
        in_specs=(P("rows", None), P("rows", "vocab"), P("rows", "vocab")),
        out_specs=(P("rows"), P("rows", None), P("rows", "vocab")),
        check_vma=False,
    )
```

```python
import functools
import math
import jax
import jax.numpy as jnp
from jax import lax
from jax.experimental import pallas as pl
from jax.experimental.pallas import tpu as pltpu
from jax.sharding import PartitionSpec as P

SIDE = 4
PLANE = SIDE * SIDE
CHIPS = SIDE * PLANE
SWAP = ((0, 1), (1, 0))
BOTH = ("rows", "vocab")
PLANES = [[c * PLANE + i for i in range(PLANE)] for c in range(SIDE)] + [
    [CHIPS + i * SIDE + c for i in range(PLANE)] for c in range(SIDE)
]
TOKENS_PIECE = 16
COLS_PIECE = 512
BLOCK = 640
LOG2E = math.log2(math.e)
F32, BF16 = jnp.float32, jnp.bfloat16
VMEM = pl.BlockSpec(memory_space=pltpu.VMEM)
HBM = pl.BlockSpec(memory_space=pltpu.HBM)
ANY = pl.BlockSpec(memory_space=pl.ANY)


def dot(a, b, ca, cb):
    return lax.dot_general(a, b, (((ca,), (cb,)), ((), ())), preferred_element_type=F32)


def swap(x):
    return lax.ppermute(x, "rows", SWAP)


def shift(k):
    return [(PLANES[r + c][i], PLANES[r + (c + k) % SIDE][i]) for r in (0, SIDE) for c in range(SIDE) for i in range(PLANE)]


def params(mib):
    return pltpu.CompilerParams(vmem_limit_bytes=mib * 1024 * 1024)


def cost(flops, moved):
    return pl.CostEstimate(flops=flops, bytes_accessed=moved, transcendentals=0)


def exp(x):
    return jnp.exp2(x * LOG2E)


def blocks(n):
    return [(c, min(c + BLOCK, n)) for c in range(0, n, BLOCK)]


def tiles(x):
    return [x[:, c : c + 128] for c in range(0, x.shape[1], 128)]


def stat_rows(tokens):
    return pl.cdiv(3 * tokens // 128, 8) * 8


def load(source, target, sems):
    copies = []
    for j, (c, e) in enumerate(blocks(source.shape[1])):
        part = pl.ds(c, e - c)
        copies.append(pltpu.make_async_copy(source.at[:, part], target.at[:, part], sems.at[j]))
        copies[-1].start()
    return copies


def own_kernel(mine, target, weight, acc, probs, stat, buffer, sems):
    vocab = target.shape[1]
    copies = load(weight, buffer, sems)
    wide = target[...].astype(F32)
    peak = jnp.max(wide, axis=1, keepdims=True)
    terms = exp(wide - peak)
    total = jnp.sum(terms, axis=1, keepdims=True)
    terms = terms / total
    probs[...] = terms
    mean = jnp.sum(terms * wide, axis=1, keepdims=True)
    lane = lax.broadcasted_iota(jnp.int32, stat.shape, 1)
    stat[...] = jnp.where(lane == 0, peak + jnp.log(total), mean)
    for copy, (c, e) in zip(copies, blocks(vocab)):
        copy.wait()
        acc[:, c:e] = dot(mine[...], buffer[:, c:e], 1, 0)


def own_part(mine, target, weight):
    tokens, half = mine.shape
    vocab = target.shape[1]
    return pl.pallas_call(
        own_kernel,
        in_specs=[VMEM] * 2 + [ANY],
        out_specs=[VMEM] * 4,
        out_shape=[
            jax.ShapeDtypeStruct((tokens, vocab), F32),
            jax.ShapeDtypeStruct((tokens, vocab), F32),
            jax.ShapeDtypeStruct((tokens, 128), F32),
            jax.ShapeDtypeStruct((half, vocab), BF16),
        ],
        scratch_shapes=[pltpu.SemaphoreType.DMA((len(blocks(vocab)),))],
        compiler_params=params(16),
        cost_estimate=cost(2 * tokens * half * vocab, 2 * half * vocab),
        name="own_part",
    )(mine, target, weight)


def draft_kernel(theirs, acc, probs, stat, weight, draft, out, buffer, sems):
    tokens, vocab = draft.shape
    copies = load(weight, buffer, sems)
    peak = jnp.full((tokens, 128), -jnp.inf, F32)
    cross = jnp.zeros((tokens, 128), F32)
    for j, (c, e) in enumerate(blocks(vocab)):
        copies[j].wait()
        value = acc[:, c:e] + dot(theirs[...], buffer[:, c:e], 1, 0)
        draft[:, c:e] = value
        for tile, weighed in zip(tiles(value), tiles(probs[:, c:e] * value)):
            peak = jnp.maximum(peak, tile)
            cross = cross + weighed
    top = jnp.max(peak, axis=1, keepdims=True)
    total = jnp.zeros((tokens, 128), F32)
    for tile in tiles(draft[...]):
        total = total + exp(tile - top)
    lse_q = top + jnp.log(jnp.sum(total, axis=1, keepdims=True))
    mean = stat[:, 1:2] - jnp.sum(cross, axis=1, keepdims=True)
    lane = lax.broadcasted_iota(jnp.int32, stat.shape, 1)
    rows = jnp.where(lane == 0, stat[:, :1], jnp.where(lane == 1, mean, lse_q)).T
    out[...] = jnp.zeros(out.shape, F32)
    for i in range(3):
        for k in range(tokens // 128):
            at = i * (tokens // 128) + k
            out[at : at + 1] = rows[i : i + 1, k * 128 : (k + 1) * 128]


def draft_part(theirs, acc, probs, stat, weight):
    tokens, half = theirs.shape
    vocab = acc.shape[1]
    steps = len(blocks(vocab))
    return pl.pallas_call(
        draft_kernel,
        in_specs=[VMEM] * 4 + [ANY],
        out_specs=[VMEM] * 3,
        out_shape=[
            jax.ShapeDtypeStruct((tokens, vocab), F32),
            jax.ShapeDtypeStruct((stat_rows(tokens), 128), F32),
            jax.ShapeDtypeStruct((half, vocab), BF16),
        ],
        scratch_shapes=[pltpu.SemaphoreType.DMA((steps,))],
        compiler_params=params(20),
        cost_estimate=cost(2 * tokens * half * vocab, 2 * half * vocab),
        name="draft_part",
    )(theirs, acc, probs, stat, weight)


def back_kernel(factor, row, parts, draft, target, weight, weight_o, divergence, dlogits, out):
    lines = draft.shape[0] // 128
    every = parts[...]
    top = jnp.max(every, axis=0)
    scale = exp(every - top)
    lse = top + jnp.log(jnp.sum(scale, axis=0))
    cross = jnp.sum(scale[:, :lines] * every[:, lines : 2 * lines], axis=0)
    mean = cross / jnp.sum(scale[:, :lines], axis=0)
    result = mean - lse[:lines] + lse[2 * lines : 3 * lines]
    for k in range(lines):
        divergence[:, k * 128 : (k + 1) * 128] = result[k : k + 1]
    turned = jnp.concatenate([lse, jnp.zeros((128 - lse.shape[0], 128), F32)], axis=0).T
    lse_t = jnp.concatenate([turned[:, k : k + 1] for k in range(lines)], axis=0)
    lse_q = jnp.concatenate([turned[:, 2 * lines + k : 2 * lines + k + 1] for k in range(lines)], axis=0)

    half = weight.shape[0]
    per = half // COLS_PIECE
    down = dlogits.shape[0] // TOKENS_PIECE
    sums = [None] * (2 * per)
    for c, e in blocks(draft.shape[1]):
        probs_q = exp(draft[:, c:e] - lse_q)
        probs_t = exp(target[:, c:e].astype(F32) - lse_t)
        block = ((probs_q - probs_t) * factor).astype(BF16)
        dlogits[:, c:e] = block
        for j in range(2 * per):
            rows = pl.ds(j % per * COLS_PIECE, COLS_PIECE)
            term = dot(block, (weight, weight_o)[j // per][rows, c:e], 1, 1)
            sums[j] = term if sums[j] is None else sums[j] + term
    along, across = jnp.where(row[0] == 0, 1, SIDE), jnp.where(row[0] == 0, PLANE, 1)
    for j in range(2 * per):
        first = lax.rem(row[0] * per + j, 2 * per) * across
        total = sums[j].astype(BF16)
        for i in range(down):
            out[first + i * along] = total[i * TOKENS_PIECE : (i + 1) * TOKENS_PIECE]


def back_part(factor, row, parts, draft, target, weight, weight_o):
    tokens, vocab = draft.shape
    half = weight.shape[0]
    pieces = (tokens // TOKENS_PIECE) * (2 * half // COLS_PIECE)
    return pl.pallas_call(
        functools.partial(back_kernel, factor),
        in_specs=[pl.BlockSpec(memory_space=pltpu.SMEM)] + [VMEM] * 5,
        out_specs=[VMEM] * 3,
        out_shape=[
            jax.ShapeDtypeStruct((1, tokens), F32),
            jax.ShapeDtypeStruct((tokens, vocab), BF16),
            jax.ShapeDtypeStruct((pieces, TOKENS_PIECE, COLS_PIECE), BF16),
        ],
        compiler_params=params(16),
        cost_estimate=cost(4 * tokens * half * vocab, 4 * half * vocab),
        name="back_part",
    )(row, parts, draft, target, weight, weight_o)


def sum_kernel(terms, out):
    total = terms[0].astype(F32)
    for i in range(1, terms.shape[0]):
        total = total + terms[i].astype(F32)
    out[...] = jnp.broadcast_to(total.astype(BF16)[None], out.shape)


def sum_part(terms):
    return pl.pallas_call(
        sum_kernel,
        in_specs=[VMEM],
        out_specs=VMEM,
        out_shape=jax.ShapeDtypeStruct((PLANE,) + terms.shape[1:], BF16),
        compiler_params=params(8),
        name="sum_part",
    )(terms)


def join_kernel(own, *rest):
    *pieces, out, stage, sems = rest
    copies = []
    for k, piece in enumerate(pieces):
        stage[k] = piece[...].reshape(stage.shape[1:]).astype(F32)
        column = pl.multiple_of(lax.rem(own[0] + SIDE - k, SIDE) * COLS_PIECE, COLS_PIECE)
        copies.append(pltpu.make_async_copy(stage.at[k], out.at[:, pl.ds(column, COLS_PIECE)], sems.at[k]))
        copies[-1].start()
    for copy in copies:
        copy.wait()


def join_part(own, pieces, tokens, width):
    return pl.pallas_call(
        join_kernel,
        in_specs=[pl.BlockSpec(memory_space=pltpu.SMEM)] + [VMEM] * SIDE,
        out_specs=ANY,
        out_shape=jax.ShapeDtypeStruct((tokens, width), F32),
        scratch_shapes=[pltpu.VMEM((SIDE, tokens, COLS_PIECE), F32), pltpu.SemaphoreType.DMA((SIDE,))],
        compiler_params=params(8),
        name="join_part",
    )(own, *pieces)


def head_kernel(mine, mine_o, dlogits, dlogits_o, out):
    out[...] = dot(mine[...], dlogits[...], 0, 0) + dot(mine_o[...], dlogits_o[...], 0, 0)


def head_part(mine, mine_o, dlogits, dlogits_o):
    tokens, half = mine.shape
    vocab = dlogits.shape[1]
    step = 128
    column = pl.BlockSpec((tokens, step), lambda j: (0, j))
    return pl.pallas_call(
        head_kernel,
        grid=(half // step,),
        in_specs=[column, column, VMEM, VMEM],
        out_specs=pl.BlockSpec((step, vocab), lambda j: (j, 0)),
        out_shape=jax.ShapeDtypeStruct((half, vocab), F32),
        compiler_params=params(16),
        cost_estimate=cost(4 * tokens * half * vocab, 4 * half * vocab),
        name="head_part",
    )(mine, mine_o, dlogits, dlogits_o)


def shards(hidden, weight, target):
    n = lax.axis_size("vocab")
    row = lax.axis_index("rows")
    tokens, width = hidden.shape
    half, vocab = weight.shape

    with jax.named_scope("swap_weight"):
        weight_o = swap(weight)
    mine = lax.dynamic_slice_in_dim(hidden, row * half, half, 1)
    theirs = lax.dynamic_slice_in_dim(hidden, (1 - row) * half, half, 1)

    acc, probs, stat, weight_v = own_part(mine, target, weight)
    draft, part, weight_o = draft_part(theirs, acc, probs, stat, weight_o)
    with jax.named_scope("share_stats"):
        parts = lax.all_to_all(jnp.broadcast_to(part[None], (n,) + part.shape), "vocab", 0, 0)
    divergence, dlogits, pieces = back_part(
        vocab * n / 1024.0, jnp.full((1,), row, jnp.int32), parts, draft, target, weight_v, weight_o
    )
    with jax.named_scope("scatter_sum"):
        terms = lax.all_to_all(pieces, "vocab", 0, 0)
    totals = sum_part(terms)
    with jax.named_scope("gather_plane"):
        plane = lax.all_to_all(totals, BOTH, 0, 0, axis_index_groups=PLANES)
    dlogits, theirs, plane = lax.optimization_barrier((dlogits, theirs, plane))
    with jax.named_scope("gather_planes"):
        planes = [plane] + [lax.ppermute(plane, BOTH, shift(k)) for k in range(1, SIDE)]
    with jax.named_scope("swap_back"):
        mine_o, dlogits_o = swap(theirs), swap(dlogits)
    head_grad = head_part(mine, mine_o, dlogits, dlogits_o)
    *planes, head_grad = lax.optimization_barrier((*planes, head_grad))
    chip = lax.axis_index("vocab")
    own = jnp.where(row == 0, chip // PLANE, chip % SIDE).astype(jnp.int32)
    hidden_grad = join_part(own.reshape(1), planes, tokens, width)
    return (divergence.reshape(tokens), hidden_grad, head_grad)


def solution(mesh):
    return jax.shard_map(
        shards,
        mesh=mesh,
        in_specs=(P("rows", None), P("rows", "vocab"), P("rows", "vocab")),
        out_specs=(P("rows"), P("rows", None), P("rows", "vocab")),
        check_vma=False,
    )
```

```python
import functools
import math
import jax
import jax.numpy as jnp
from jax import lax
from jax.experimental import pallas as pl
from jax.experimental.pallas import tpu as pltpu
from jax.sharding import PartitionSpec as P

SIDE = 4
PLANE = SIDE * SIDE
CHIPS = SIDE * PLANE
SWAP = ((0, 1), (1, 0))
BOTH = ("rows", "vocab")
PLANES = [[c * PLANE + i for i in range(PLANE)] for c in range(SIDE)] + [
    [CHIPS + i * SIDE + c for i in range(PLANE)] for c in range(SIDE)
]
TOKENS_PIECE = 16
COLS_PIECE = 512
BLOCK = 640
LOG2E = math.log2(math.e)
F32, BF16 = jnp.float32, jnp.bfloat16
VMEM = pl.BlockSpec(memory_space=pltpu.VMEM)
HBM = pl.BlockSpec(memory_space=pltpu.HBM)
ANY = pl.BlockSpec(memory_space=pl.ANY)


def dot(a, b, ca, cb):
    return lax.dot_general(a, b, (((ca,), (cb,)), ((), ())), preferred_element_type=F32)


def swap(x):
    return lax.ppermute(x, "rows", SWAP)


def shift(k):
    return [(PLANES[r + c][i], PLANES[r + (c + k) % SIDE][i]) for r in (0, SIDE) for c in range(SIDE) for i in range(PLANE)]


def params(mib):
    return pltpu.CompilerParams(vmem_limit_bytes=mib * 1024 * 1024)


def cost(flops, moved):
    return pl.CostEstimate(flops=flops, bytes_accessed=moved, transcendentals=0)


def exp(x):
    return jnp.exp2(x * LOG2E)


def blocks(n):
    return [(c, min(c + BLOCK, n)) for c in range(0, n, BLOCK)]


def tiles(x):
    return [x[:, c : c + 128] for c in range(0, x.shape[1], 128)]


def stat_rows(tokens):
    return pl.cdiv(3 * tokens // 128, 8) * 8


def load(source, target, sems):
    copies = []
    for j, (c, e) in enumerate(blocks(source.shape[1])):
        part = pl.ds(c, e - c)
        copies.append(pltpu.make_async_copy(source.at[:, part], target.at[:, part], sems.at[j]))
        copies[-1].start()
    return copies


def own_kernel(mine, target, weight, acc, probs, stat, buffer, sems):
    vocab = target.shape[1]
    copies = load(weight, buffer, sems)
    wide = target[...].astype(F32)
    peak = jnp.max(wide, axis=1, keepdims=True)
    terms = exp(wide - peak)
    total = jnp.sum(terms, axis=1, keepdims=True)
    terms = terms / total
    probs[...] = terms
    mean = jnp.sum(terms * wide, axis=1, keepdims=True)
    lane = lax.broadcasted_iota(jnp.int32, stat.shape, 1)
    stat[...] = jnp.where(lane == 0, peak + jnp.log(total), mean)
    for copy, (c, e) in zip(copies, blocks(vocab)):
        copy.wait()
        acc[:, c:e] = dot(mine[...], buffer[:, c:e], 1, 0)


def own_part(mine, target, weight):
    tokens, half = mine.shape
    vocab = target.shape[1]
    return pl.pallas_call(
        own_kernel,
        in_specs=[VMEM] * 2 + [ANY],
        out_specs=[VMEM] * 4,
        out_shape=[
            jax.ShapeDtypeStruct((tokens, vocab), F32),
            jax.ShapeDtypeStruct((tokens, vocab), F32),
            jax.ShapeDtypeStruct((tokens, 128), F32),
            jax.ShapeDtypeStruct((half, vocab), BF16),
        ],
        scratch_shapes=[pltpu.SemaphoreType.DMA((len(blocks(vocab)),))],
        compiler_params=params(16),
        cost_estimate=cost(2 * tokens * half * vocab, 2 * half * vocab),
        name="own_part",
    )(mine, target, weight)


def draft_kernel(theirs, acc, probs, stat, weight, draft, out, buffer, sems):
    tokens, vocab = draft.shape
    copies = load(weight, buffer, sems)
    peak = jnp.full((tokens, 128), -jnp.inf, F32)
    cross = jnp.zeros((tokens, 128), F32)
    for j, (c, e) in enumerate(blocks(vocab)):
        copies[j].wait()
        value = acc[:, c:e] + dot(theirs[...], buffer[:, c:e], 1, 0)
        draft[:, c:e] = value
        for tile, weighed in zip(tiles(value), tiles(probs[:, c:e] * value)):
            peak = jnp.maximum(peak, tile)
            cross = cross + weighed
    top = jnp.max(peak, axis=1, keepdims=True)
    total = jnp.zeros((tokens, 128), F32)
    for tile in tiles(draft[...]):
        total = total + exp(tile - top)
    lse_q = top + jnp.log(jnp.sum(total, axis=1, keepdims=True))
    mean = stat[:, 1:2] - jnp.sum(cross, axis=1, keepdims=True)
    lane = lax.broadcasted_iota(jnp.int32, stat.shape, 1)
    rows = jnp.where(lane == 0, stat[:, :1], jnp.where(lane == 1, mean, lse_q)).T
    out[...] = jnp.zeros(out.shape, F32)
    for i in range(3):
        for k in range(tokens // 128):
            at = i * (tokens // 128) + k
            out[at : at + 1] = rows[i : i + 1, k * 128 : (k + 1) * 128]


def draft_part(theirs, acc, probs, stat, weight):
    tokens, half = theirs.shape
    vocab = acc.shape[1]
    steps = len(blocks(vocab))
    return pl.pallas_call(
        draft_kernel,
        in_specs=[VMEM] * 4 + [ANY],
        out_specs=[VMEM] * 3,
        out_shape=[
            jax.ShapeDtypeStruct((tokens, vocab), F32),
            jax.ShapeDtypeStruct((stat_rows(tokens), 128), F32),
            jax.ShapeDtypeStruct((half, vocab), BF16),
        ],
        scratch_shapes=[pltpu.SemaphoreType.DMA((steps,))],
        compiler_params=params(20),
        cost_estimate=cost(2 * tokens * half * vocab, 2 * half * vocab),
        name="draft_part",
    )(theirs, acc, probs, stat, weight)


def back_kernel(factor, row, parts, draft, target, weight, weight_o, divergence, dlogits, out):
    lines = draft.shape[0] // 128
    every = parts[...]
    top = jnp.max(every, axis=0)
    scale = exp(every - top)
    lse = top + jnp.log(jnp.sum(scale, axis=0))
    cross = jnp.sum(scale[:, :lines] * every[:, lines : 2 * lines], axis=0)
    mean = cross / jnp.sum(scale[:, :lines], axis=0)
    result = mean - lse[:lines] + lse[2 * lines : 3 * lines]
    for k in range(lines):
        divergence[:, k * 128 : (k + 1) * 128] = result[k : k + 1]
    turned = jnp.concatenate([lse, jnp.zeros((128 - lse.shape[0], 128), F32)], axis=0).T
    lse_t = jnp.concatenate([turned[:, k : k + 1] for k in range(lines)], axis=0)
    lse_q = jnp.concatenate([turned[:, 2 * lines + k : 2 * lines + k + 1] for k in range(lines)], axis=0)

    half = weight.shape[0]
    per = half // COLS_PIECE
    down = dlogits.shape[0] // TOKENS_PIECE
    sums = [None] * (2 * per)
    for c, e in blocks(draft.shape[1]):
        probs_q = exp(draft[:, c:e] - lse_q)
        probs_t = exp(target[:, c:e].astype(F32) - lse_t)
        block = ((probs_q - probs_t) * factor).astype(BF16)
        dlogits[:, c:e] = block
        for j in range(2 * per):
            rows = pl.ds(j % per * COLS_PIECE, COLS_PIECE)
            term = dot(block, (weight, weight_o)[j // per][rows, c:e], 1, 1)
            sums[j] = term if sums[j] is None else sums[j] + term
    along, across = jnp.where(row[0] == 0, 1, SIDE), jnp.where(row[0] == 0, PLANE, 1)
    for j in range(2 * per):
        first = lax.rem(row[0] * per + j, 2 * per) * across
        total = sums[j].astype(BF16)
        for i in range(down):
            out[first + i * along] = total[i * TOKENS_PIECE : (i + 1) * TOKENS_PIECE]


def back_part(factor, row, parts, draft, target, weight, weight_o):
    tokens, vocab = draft.shape
    half = weight.shape[0]
    pieces = (tokens // TOKENS_PIECE) * (2 * half // COLS_PIECE)
    return pl.pallas_call(
        functools.partial(back_kernel, factor),
        in_specs=[pl.BlockSpec(memory_space=pltpu.SMEM)] + [VMEM] * 5,
        out_specs=[VMEM] * 3,
        out_shape=[
            jax.ShapeDtypeStruct((1, tokens), F32),
            jax.ShapeDtypeStruct((tokens, vocab), BF16),
            jax.ShapeDtypeStruct((pieces, TOKENS_PIECE, COLS_PIECE), BF16),
        ],
        compiler_params=params(16),
        cost_estimate=cost(4 * tokens * half * vocab, 4 * half * vocab),
        name="back_part",
    )(row, parts, draft, target, weight, weight_o)


def sum_kernel(terms, out):
    total = terms[0].astype(F32)
    for i in range(1, terms.shape[0]):
        total = total + terms[i].astype(F32)
    out[...] = jnp.broadcast_to(total.astype(BF16)[None], out.shape)


def sum_part(terms):
    return pl.pallas_call(
        sum_kernel,
        in_specs=[VMEM],
        out_specs=VMEM,
        out_shape=jax.ShapeDtypeStruct((PLANE,) + terms.shape[1:], BF16),
        compiler_params=params(8),
        name="sum_part",
    )(terms)


def join_kernel(own, *rest):
    *pieces, out, held, stage, sems, out_sems = rest
    loads = [pltpu.make_async_copy(piece, held.at[k], sems.at[k]) for k, piece in enumerate(pieces)]
    for each in loads:
        each.start()
    copies = []
    for k, each in enumerate(loads):
        each.wait()
        stage[k] = held[k].reshape(stage.shape[1:]).astype(F32)
        column = pl.multiple_of(lax.rem(own[0] + SIDE - k, SIDE) * COLS_PIECE, COLS_PIECE)
        copies.append(pltpu.make_async_copy(stage.at[k], out.at[:, pl.ds(column, COLS_PIECE)], out_sems.at[k]))
        copies[-1].start()
    for copy in copies:
        copy.wait()


def join_part(own, pieces, tokens, width):
    return pl.pallas_call(
        join_kernel,
        in_specs=[pl.BlockSpec(memory_space=pltpu.SMEM)] + [ANY] * SIDE,
        out_specs=ANY,
        out_shape=jax.ShapeDtypeStruct((tokens, width), F32),
        scratch_shapes=[
            pltpu.VMEM((SIDE, PLANE, TOKENS_PIECE, COLS_PIECE), BF16),
            pltpu.VMEM((SIDE, tokens, COLS_PIECE), F32),
            pltpu.SemaphoreType.DMA((SIDE,)),
            pltpu.SemaphoreType.DMA((SIDE,)),
        ],
        compiler_params=params(8),
        name="join_part",
    )(own, *pieces)


def head_kernel(mine, dlogits, mine_o, dlogits_o, out, held, held_o, stage, sems, out_sems):
    steps, step = stage.shape[:2]
    loads = [pltpu.make_async_copy(*pair) for pair in ((mine_o, held, sems.at[0]), (dlogits_o, held_o, sems.at[1]))]
    for each in loads:
        each.start()
    copies = []
    for j in range(steps):
        part = pl.ds(j * step, step)
        value = dot(mine[:, part], dlogits[...], 0, 0)
        if j == 0:
            for each in loads:
                each.wait()
        stage[j] = value + dot(held[:, part], held_o[...], 0, 0)
        copies.append(pltpu.make_async_copy(stage.at[j], out.at[part], out_sems.at[j]))
        copies[-1].start()
    for copy in copies:
        copy.wait()


def head_part(mine, mine_o, dlogits, dlogits_o):
    tokens, half = mine.shape
    vocab = dlogits.shape[1]
    step = 128
    return pl.pallas_call(
        head_kernel,
        in_specs=[VMEM] * 2 + [ANY] * 2,
        out_specs=ANY,
        out_shape=jax.ShapeDtypeStruct((half, vocab), F32),
        scratch_shapes=[
            pltpu.VMEM((tokens, half), BF16),
            pltpu.VMEM((tokens, vocab), BF16),
            pltpu.VMEM((half // step, step, vocab), F32),
            pltpu.SemaphoreType.DMA((2,)),
            pltpu.SemaphoreType.DMA((half // step,)),
        ],
        compiler_params=params(24),
        cost_estimate=cost(4 * tokens * half * vocab, 4 * half * vocab),
        name="head_part",
    )(mine, dlogits, mine_o, dlogits_o)


def shards(hidden, weight, target):
    n = lax.axis_size("vocab")
    row = lax.axis_index("rows")
    tokens, width = hidden.shape
    half, vocab = weight.shape

    with jax.named_scope("swap_weight"):
        weight_o = swap(weight)
    mine = lax.dynamic_slice_in_dim(hidden, row * half, half, 1)
    theirs = lax.dynamic_slice_in_dim(hidden, (1 - row) * half, half, 1)

    acc, probs, stat, weight_v = own_part(mine, target, weight)
    draft, part, weight_o = draft_part(theirs, acc, probs, stat, weight_o)
    theirs, part = lax.optimization_barrier((theirs, part))
    with jax.named_scope("swap_hidden"):
        mine_o = swap(theirs)
    with jax.named_scope("share_stats"):
        parts = lax.all_to_all(jnp.broadcast_to(part[None], (n,) + part.shape), "vocab", 0, 0)
    divergence, dlogits, pieces = back_part(
        vocab * n / 1024.0, jnp.full((1,), row, jnp.int32), parts, draft, target, weight_v, weight_o
    )
    pieces, mine_o = lax.optimization_barrier((pieces, mine_o))
    with jax.named_scope("scatter_sum"):
        terms = lax.all_to_all(pieces, "vocab", 0, 0)
    totals = sum_part(terms)
    with jax.named_scope("gather_plane"):
        plane = lax.all_to_all(totals, BOTH, 0, 0, axis_index_groups=PLANES)
    dlogits, plane = lax.optimization_barrier((dlogits, plane))
    with jax.named_scope("gather_planes"):
        planes = [plane] + [lax.ppermute(plane, BOTH, shift(k)) for k in range(1, SIDE)]
    with jax.named_scope("swap_dlogits"):
        dlogits_o = swap(dlogits)
    head_grad = head_part(mine, mine_o, dlogits, dlogits_o)
    *planes, head_grad = lax.optimization_barrier((*planes, head_grad))
    chip = lax.axis_index("vocab")
    own = jnp.where(row == 0, chip // PLANE, chip % SIDE).astype(jnp.int32)
    hidden_grad = join_part(own.reshape(1), planes, tokens, width)
    return (divergence.reshape(tokens), hidden_grad, head_grad)


def solution(mesh):
    return jax.shard_map(
        shards,
        mesh=mesh,
        in_specs=(P("rows", None), P("rows", "vocab"), P("rows", "vocab")),
        out_specs=(P("rows"), P("rows", None), P("rows", "vocab")),
        check_vma=False,
    )
```

```python
import functools
import math
import jax
import jax.numpy as jnp
from jax import lax
from jax.experimental import pallas as pl
from jax.experimental.pallas import tpu as pltpu
from jax.sharding import PartitionSpec as P

SWAP = ((0, 1), (1, 0))
TOKENS_PIECE = 16
COLS_PIECE = 512
BLOCK = 640
LOG2E = math.log2(math.e)
F32, BF16 = jnp.float32, jnp.bfloat16
VMEM = pl.BlockSpec(memory_space=pltpu.VMEM)
HBM = pl.BlockSpec(memory_space=pltpu.HBM)
ANY = pl.BlockSpec(memory_space=pl.ANY)


def dot(a, b, ca, cb):
    return lax.dot_general(a, b, (((ca,), (cb,)), ((), ())), preferred_element_type=F32)


def swap(x):
    return lax.ppermute(x, "rows", SWAP)


def params(mib):
    return pltpu.CompilerParams(vmem_limit_bytes=mib * 1024 * 1024)


def cost(flops, moved):
    return pl.CostEstimate(flops=flops, bytes_accessed=moved, transcendentals=0)


def exp(x):
    return jnp.exp2(x * LOG2E)


def blocks(n):
    return [(c, min(c + BLOCK, n)) for c in range(0, n, BLOCK)]


def thirds(n):
    step = pl.cdiv(n // 128, 3) * 128
    return [(c, min(c + step, n)) for c in range(0, n, step)]


def tiles(x):
    return [x[:, c : c + 128] for c in range(0, x.shape[1], 128)]


def stat_rows(tokens):
    return pl.cdiv(3 * tokens // 128, 8) * 8


def load(source, target, sems):
    copies = []
    for j, (c, e) in enumerate(blocks(source.shape[1])):
        part = pl.ds(c, e - c)
        copies.append(pltpu.make_async_copy(source.at[:, part], target.at[:, part], sems.at[j]))
        copies[-1].start()
    return copies


def own_kernel(mine, target, weight, acc, probs, stat, buffer, sems):
    vocab = target.shape[1]
    copies = load(weight, buffer, sems)
    wide = target[...].astype(F32)
    peak = jnp.max(wide, axis=1, keepdims=True)
    terms = exp(wide - peak)
    total = jnp.sum(terms, axis=1, keepdims=True)
    terms = terms / total
    probs[...] = terms
    mean = jnp.sum(terms * wide, axis=1, keepdims=True)
    lane = lax.broadcasted_iota(jnp.int32, stat.shape, 1)
    stat[...] = jnp.where(lane == 0, peak + jnp.log(total), mean)
    for copy, (c, e) in zip(copies, blocks(vocab)):
        copy.wait()
        acc[:, c:e] = dot(mine[...], buffer[:, c:e], 1, 0)


def own_part(mine, target, weight):
    tokens, half = mine.shape
    vocab = target.shape[1]
    return pl.pallas_call(
        own_kernel,
        in_specs=[VMEM] * 2 + [ANY],
        out_specs=[VMEM] * 4,
        out_shape=[
            jax.ShapeDtypeStruct((tokens, vocab), F32),
            jax.ShapeDtypeStruct((tokens, vocab), F32),
            jax.ShapeDtypeStruct((tokens, 128), F32),
            jax.ShapeDtypeStruct((half, vocab), BF16),
        ],
        scratch_shapes=[pltpu.SemaphoreType.DMA((len(blocks(vocab)),))],
        compiler_params=params(16),
        cost_estimate=cost(2 * tokens * half * vocab, 2 * half * vocab),
        name="own_part",
    )(mine, target, weight)


def draft_kernel(theirs, acc, probs, stat, weight, draft, out, buffer, sems):
    tokens, vocab = draft.shape
    copies = load(weight, buffer, sems)
    peak = jnp.full((tokens, 128), -jnp.inf, F32)
    cross = jnp.zeros((tokens, 128), F32)
    for j, (c, e) in enumerate(blocks(vocab)):
        copies[j].wait()
        value = acc[:, c:e] + dot(theirs[...], buffer[:, c:e], 1, 0)
        draft[:, c:e] = value
        for tile, weighed in zip(tiles(value), tiles(probs[:, c:e] * value)):
            peak = jnp.maximum(peak, tile)
            cross = cross + weighed
    top = jnp.max(peak, axis=1, keepdims=True)
    total = jnp.zeros((tokens, 128), F32)
    for tile in tiles(draft[...]):
        total = total + exp(tile - top)
    lse_q = top + jnp.log(jnp.sum(total, axis=1, keepdims=True))
    mean = stat[:, 1:2] - jnp.sum(cross, axis=1, keepdims=True)
    lane = lax.broadcasted_iota(jnp.int32, stat.shape, 1)
    rows = jnp.where(lane == 0, stat[:, :1], jnp.where(lane == 1, mean, lse_q)).T
    out[...] = jnp.zeros(out.shape, F32)
    for i in range(3):
        for k in range(tokens // 128):
            at = i * (tokens // 128) + k
            out[at : at + 1] = rows[i : i + 1, k * 128 : (k + 1) * 128]


def draft_part(theirs, acc, probs, stat, weight):
    tokens, half = theirs.shape
    vocab = acc.shape[1]
    steps = len(blocks(vocab))
    return pl.pallas_call(
        draft_kernel,
        in_specs=[VMEM] * 4 + [ANY],
        out_specs=[VMEM] * 3,
        out_shape=[
            jax.ShapeDtypeStruct((tokens, vocab), F32),
            jax.ShapeDtypeStruct((stat_rows(tokens), 128), F32),
            jax.ShapeDtypeStruct((half, vocab), BF16),
        ],
        scratch_shapes=[pltpu.SemaphoreType.DMA((steps,))],
        compiler_params=params(20),
        cost_estimate=cost(2 * tokens * half * vocab, 2 * half * vocab),
        name="draft_part",
    )(theirs, acc, probs, stat, weight)


def back_kernel(factor, row, parts, draft, target, weight, weight_o, divergence, out, *dlogits):
    lines = draft.shape[0] // 128
    every = parts[...]
    top = jnp.max(every, axis=0)
    scale = exp(every - top)
    lse = top + jnp.log(jnp.sum(scale, axis=0))
    cross = jnp.sum(scale[:, :lines] * every[:, lines : 2 * lines], axis=0)
    mean = cross / jnp.sum(scale[:, :lines], axis=0)
    result = mean - lse[:lines] + lse[2 * lines : 3 * lines]
    for k in range(lines):
        divergence[:, k * 128 : (k + 1) * 128] = result[k : k + 1]
    turned = jnp.concatenate([lse, jnp.zeros((128 - lse.shape[0], 128), F32)], axis=0).T
    lse_t = jnp.concatenate([turned[:, k : k + 1] for k in range(lines)], axis=0)
    lse_q = jnp.concatenate([turned[:, 2 * lines + k : 2 * lines + k + 1] for k in range(lines)], axis=0)

    half = weight.shape[0]
    per = half // COLS_PIECE
    down = draft.shape[0] // TOKENS_PIECE
    sums = [None] * (2 * per)
    for kept, (c, e) in zip(dlogits, thirds(draft.shape[1])):
        probs_q = exp(draft[:, c:e] - lse_q)
        probs_t = exp(target[:, c:e].astype(F32) - lse_t)
        block = ((probs_q - probs_t) * factor).astype(BF16)
        kept[...] = block
        for j in range(2 * per):
            rows = pl.ds(j % per * COLS_PIECE, COLS_PIECE)
            term = dot(block, (weight, weight_o)[j // per][rows, c:e], 1, 1)
            sums[j] = term if sums[j] is None else sums[j] + term
    for j in range(2 * per):
        place = lax.rem(row[0] * per + j, 2 * per)
        out[pl.ds(place * down, down)] = sums[j].astype(BF16).reshape(down, TOKENS_PIECE, COLS_PIECE)


def back_part(factor, row, parts, draft, target, weight, weight_o):
    tokens, vocab = draft.shape
    half = weight.shape[0]
    pieces = (tokens // TOKENS_PIECE) * (2 * half // COLS_PIECE)
    return pl.pallas_call(
        functools.partial(back_kernel, factor),
        in_specs=[pl.BlockSpec(memory_space=pltpu.SMEM)] + [VMEM] * 5,
        out_specs=[VMEM] * 5,
        out_shape=[
            jax.ShapeDtypeStruct((1, tokens), F32),
            jax.ShapeDtypeStruct((pieces, TOKENS_PIECE, COLS_PIECE), BF16),
        ]
        + [jax.ShapeDtypeStruct((tokens, e - c), BF16) for c, e in thirds(vocab)],
        compiler_params=params(16),
        cost_estimate=cost(4 * tokens * half * vocab, 4 * half * vocab),
        name="back_part",
    )(row, parts, draft, target, weight, weight_o)


def sum_kernel(terms, out):
    total = terms[0].astype(F32)
    for i in range(1, terms.shape[0]):
        total = total + terms[i].astype(F32)
    out[...] = jnp.broadcast_to(total.astype(BF16)[None], out.shape)


def sum_part(terms):
    return pl.pallas_call(
        sum_kernel,
        in_specs=[VMEM],
        out_specs=VMEM,
        out_shape=jax.ShapeDtypeStruct(terms.shape, BF16),
        compiler_params=params(8),
        name="sum_part",
    )(terms)


def join_kernel(pieces, out, stage, sems):
    tokens, width = out.shape
    down = tokens // TOKENS_PIECE
    steps = sems.shape[0]
    copies = []
    for step in range(steps):
        rows = pl.ds(step * tokens // steps, tokens // steps)
        for i in range(step * down // steps, (step + 1) * down // steps):
            for j in range(width // COLS_PIECE):
                place = pl.ds(i * TOKENS_PIECE, TOKENS_PIECE), pl.ds(j * COLS_PIECE, COLS_PIECE)
                stage[place] = pieces[j * down + i].astype(F32)
        copies.append(pltpu.make_async_copy(stage.at[rows], out.at[rows], sems.at[step]))
        copies[-1].start()
    for copy in copies:
        copy.wait()


def join_part(pieces, tokens, width):
    return pl.pallas_call(
        join_kernel,
        in_specs=[VMEM],
        out_specs=ANY,
        out_shape=jax.ShapeDtypeStruct((tokens, width), F32),
        scratch_shapes=[pltpu.VMEM((tokens, width), F32), pltpu.SemaphoreType.DMA((4,))],
        compiler_params=params(8),
        name="join_part",
    )(pieces)


def head_kernel(mine, *rest):
    dlogits, (mine_o, *dlogits_o), (out, held, *held_o, stage, sems, out_sems) = rest[:3], rest[3:7], rest[7:]
    steps, step = stage.shape[:2]
    pairs = zip((mine_o, *dlogits_o), (held, *held_o))
    loads = [pltpu.make_async_copy(*pair, sems.at[i]) for i, pair in enumerate(pairs)]
    for each in loads:
        each.start()
    copies = []
    for j in range(steps):
        part = pl.ds(j * step, step)
        for i, (c, e) in enumerate(thirds(out.shape[1])):
            value = dot(mine[:, part], dlogits[i][...], 0, 0)
            if j == 0:
                for each in (loads[:2] if i == 0 else loads[i + 1 : i + 2]):
                    each.wait()
            stage[j, :, c:e] = value + dot(held[:, part], held_o[i][...], 0, 0)
        copies.append(pltpu.make_async_copy(stage.at[j], out.at[part], out_sems.at[j]))
        copies[-1].start()
    for copy in copies:
        copy.wait()


def head_part(mine, mine_o, dlogits, dlogits_o):
    tokens, half = mine.shape
    vocab = sum(x.shape[1] for x in dlogits)
    step = 128
    return pl.pallas_call(
        head_kernel,
        in_specs=[VMEM] * 4 + [ANY] * 4,
        out_specs=ANY,
        out_shape=jax.ShapeDtypeStruct((half, vocab), F32),
        scratch_shapes=[pltpu.VMEM(x.shape, BF16) for x in (mine_o, *dlogits_o)]
        + [
            pltpu.VMEM((half // step, step, vocab), F32),
            pltpu.SemaphoreType.DMA((4,)),
            pltpu.SemaphoreType.DMA((half // step,)),
        ],
        compiler_params=params(24),
        cost_estimate=cost(4 * tokens * half * vocab, 4 * half * vocab),
        name="head_part",
    )(mine, *dlogits, mine_o, *dlogits_o)


def shards(hidden, weight, target):
    n = lax.axis_size("vocab")
    row = lax.axis_index("rows")
    tokens, width = hidden.shape
    half, vocab = weight.shape

    with jax.named_scope("swap_weight"):
        weight_o = swap(weight)
    mine = lax.dynamic_slice_in_dim(hidden, row * half, half, 1)
    theirs = lax.dynamic_slice_in_dim(hidden, (1 - row) * half, half, 1)

    acc, probs, stat, weight_v = own_part(mine, target, weight)
    draft, part, weight_o = draft_part(theirs, acc, probs, stat, weight_o)
    with jax.named_scope("share_stats"):
        parts = lax.all_to_all(jnp.broadcast_to(part[None], (n,) + part.shape), "vocab", 0, 0)
    divergence, pieces, *dlogits = back_part(
        vocab * n / 1024.0, jnp.full((1,), row, jnp.int32), parts, draft, target, weight_v, weight_o
    )
    with jax.named_scope("scatter_sum"):
        terms = lax.all_to_all(pieces, "vocab", 0, 0)
    with jax.named_scope("swap_back"):
        mine_o, dlogits_o = swap(theirs), [swap(x) for x in dlogits]
    head_grad = head_part(mine, mine_o, dlogits, dlogits_o)
    terms, head_grad = lax.optimization_barrier((terms, head_grad))
    totals = sum_part(terms)
    with jax.named_scope("gather"):
        gathered = lax.all_to_all(totals, "vocab", 0, 0)
    hidden_grad = join_part(gathered, tokens, width)
    return (divergence.reshape(tokens), hidden_grad, head_grad)


def solution(mesh):
    return jax.shard_map(
        shards,
        mesh=mesh,
        in_specs=(P("rows", None), P("rows", "vocab"), P("rows", "vocab")),
        out_specs=(P("rows"), P("rows", None), P("rows", "vocab")),
        check_vma=False,
    )
```

```python
import functools
import math
import jax
import jax.numpy as jnp
from jax import lax
from jax.experimental import pallas as pl
from jax.experimental.pallas import tpu as pltpu
from jax.sharding import PartitionSpec as P

SWAP = ((0, 1), (1, 0))
TOKENS_PIECE = 16
COLS_PIECE = 512
PARTS = 4
BLOCK = 640
LOG2E = math.log2(math.e)
F32, BF16 = jnp.float32, jnp.bfloat16
VMEM = pl.BlockSpec(memory_space=pltpu.VMEM)
SMEM = pl.BlockSpec(memory_space=pltpu.SMEM)
ANY = pl.BlockSpec(memory_space=pl.ANY)


def dot(a, b, ca, cb):
    return lax.dot_general(a, b, (((ca,), (cb,)), ((), ())), preferred_element_type=F32)


def swap(x):
    return lax.ppermute(x, "rows", SWAP)


def params(mib):
    return pltpu.CompilerParams(vmem_limit_bytes=mib * 1024 * 1024)


def cost(flops, moved):
    return pl.CostEstimate(flops=flops, bytes_accessed=moved, transcendentals=0)


def exp(x):
    return jnp.exp2(x * LOG2E)


def blocks(n):
    return [(c, min(c + BLOCK, n)) for c in range(0, n, BLOCK)]


def thirds(n):
    step = pl.cdiv(n // 128, 3) * 128
    return [(c, min(c + step, n)) for c in range(0, n, step)]


def tiles(x):
    return [x[:, c : c + 128] for c in range(0, x.shape[1], 128)]


def stat_rows(tokens):
    return pl.cdiv(3 * tokens // 128, 8) * 8


def own_half(x, row, half):
    return x[:, pl.ds(pl.multiple_of(row[0] * half, 128), half)]


def cross_kernel(start, row, hidden_o, weight, out):
    half = weight.shape[0]
    out[...] = dot(own_half(hidden_o, row, half), weight[:, start : start + out.shape[1]], 1, 0)


def cross_part(row, hidden_o, weight, start, stop):
    tokens, half = hidden_o.shape[0], weight.shape[0]
    return pl.pallas_call(
        functools.partial(cross_kernel, start),
        in_specs=[SMEM] + [VMEM] * 2,
        out_specs=VMEM,
        out_shape=jax.ShapeDtypeStruct((tokens, stop - start), F32),
        compiler_params=params(8),
        cost_estimate=cost(2 * tokens * half * (stop - start), 2 * half * (stop - start)),
        name="cross_part",
    )(row, hidden_o, weight)


def own_kernel(row, hidden, target, weight, acc, probs, stat, *rest):
    *parts, sems = rest
    half, vocab = weight.shape
    rows = parts[0].shape[0]
    copies = []
    for k, part in enumerate(parts):
        copies.append(pltpu.make_async_copy(weight.at[pl.ds(k * rows, rows)], part, sems.at[k]))
        copies[-1].start()
    mine = own_half(hidden, row, half)
    for c, e in blocks(vocab):
        acc[:, c:e] = dot(mine, weight[:, c:e], 1, 0)
    wide = target[...].astype(F32)
    peak = jnp.max(wide, axis=1, keepdims=True)
    terms = exp(wide - peak)
    total = jnp.sum(terms, axis=1, keepdims=True)
    terms = terms / total
    probs[...] = terms
    mean = jnp.sum(terms * wide, axis=1, keepdims=True)
    lane = lax.broadcasted_iota(jnp.int32, stat.shape, 1)
    stat[...] = jnp.where(lane == 0, peak + jnp.log(total), mean)
    for copy in copies:
        copy.wait()


def own_part(row, hidden, target, weight):
    tokens = hidden.shape[0]
    half, vocab = weight.shape
    return pl.pallas_call(
        own_kernel,
        in_specs=[SMEM] + [VMEM] * 3,
        out_specs=[VMEM] * (3 + PARTS),
        out_shape=[
            jax.ShapeDtypeStruct((tokens, vocab), F32),
            jax.ShapeDtypeStruct((tokens, vocab), F32),
            jax.ShapeDtypeStruct((tokens, 128), F32),
        ]
        + [jax.ShapeDtypeStruct((half // PARTS, vocab), BF16)] * PARTS,
        scratch_shapes=[pltpu.SemaphoreType.DMA((PARTS,))],
        compiler_params=params(8),
        cost_estimate=cost(2 * tokens * half * vocab, 2 * half * vocab),
        name="own_part",
    )(row, hidden, target, weight)


def draft_kernel(acc, probs, stat, first, second, draft, out):
    tokens, vocab = draft.shape
    peak = jnp.full((tokens, 128), -jnp.inf, F32)
    cross = jnp.zeros((tokens, 128), F32)
    split = first.shape[1]
    for c in range(0, vocab, 128):
        other = first[:, c : c + 128] if c < split else second[:, c - split : c - split + 128]
        value = acc[:, c : c + 128] + other
        draft[:, c : c + 128] = value
        peak = jnp.maximum(peak, value)
        cross = cross + probs[:, c : c + 128] * value
    top = jnp.max(peak, axis=1, keepdims=True)
    total = jnp.zeros((tokens, 128), F32)
    for tile in tiles(draft[...]):
        total = total + exp(tile - top)
    lse_q = top + jnp.log(jnp.sum(total, axis=1, keepdims=True))
    mean = stat[:, 1:2] - jnp.sum(cross, axis=1, keepdims=True)
    lane = lax.broadcasted_iota(jnp.int32, stat.shape, 1)
    rows = jnp.where(lane == 0, stat[:, :1], jnp.where(lane == 1, mean, lse_q)).T
    out[...] = jnp.zeros(out.shape, F32)
    for i in range(3):
        for k in range(tokens // 128):
            at = i * (tokens // 128) + k
            out[at : at + 1] = rows[i : i + 1, k * 128 : (k + 1) * 128]


def draft_part(acc, probs, stat, first, second):
    tokens, vocab = acc.shape
    return pl.pallas_call(
        draft_kernel,
        in_specs=[VMEM] * 5,
        out_specs=[VMEM] * 2,
        out_shape=[
            jax.ShapeDtypeStruct((tokens, vocab), F32),
            jax.ShapeDtypeStruct((stat_rows(tokens), 128), F32),
        ],
        compiler_params=params(8),
        cost_estimate=cost(16 * tokens * vocab, 16 * tokens * vocab),
        name="draft_part",
    )(acc, probs, stat, first, second)


def back_kernel(factor, row, parts, draft, target, *rest):
    weights, (divergence, out, *dlogits) = rest[: 2 * PARTS], rest[2 * PARTS :]
    lines = draft.shape[0] // 128
    every = parts[...]
    top = jnp.max(every, axis=0)
    scale = exp(every - top)
    lse = top + jnp.log(jnp.sum(scale, axis=0))
    cross = jnp.sum(scale[:, :lines] * every[:, lines : 2 * lines], axis=0)
    mean = cross / jnp.sum(scale[:, :lines], axis=0)
    result = mean - lse[:lines] + lse[2 * lines : 3 * lines]
    for k in range(lines):
        divergence[:, k * 128 : (k + 1) * 128] = result[k : k + 1]
    turned = jnp.concatenate([lse, jnp.zeros((128 - lse.shape[0], 128), F32)], axis=0).T
    lse_t = jnp.concatenate([turned[:, k : k + 1] for k in range(lines)], axis=0)
    lse_q = jnp.concatenate([turned[:, 2 * lines + k : 2 * lines + k + 1] for k in range(lines)], axis=0)

    wide = weights[0].shape[0]
    fold = COLS_PIECE // wide
    pieces = 2 * PARTS // fold
    down = draft.shape[0] // TOKENS_PIECE
    sums = [None] * (2 * PARTS)
    for kept, (c, e) in zip(dlogits, thirds(draft.shape[1])):
        probs_q = exp(draft[:, c:e] - lse_q)
        probs_t = exp(target[:, c:e].astype(F32) - lse_t)
        block = ((probs_q - probs_t) * factor).astype(BF16)
        kept[...] = block
        for j, weight in enumerate(weights):
            term = dot(block, weight[:, c:e], 1, 1)
            sums[j] = term if sums[j] is None else sums[j] + term
    for j, total in enumerate(sums):
        place = lax.rem(row[0] * (pieces // 2) + j // fold, pieces) * down
        columns = slice(j % fold * wide, (j % fold + 1) * wide)
        out[pl.ds(place, down), :, columns] = total.astype(BF16).reshape(down, TOKENS_PIECE, wide)


def back_part(factor, row, parts, draft, target, weights):
    tokens, vocab = draft.shape
    half = PARTS * weights[0].shape[0]
    pieces = (tokens // TOKENS_PIECE) * (2 * half // COLS_PIECE)
    return pl.pallas_call(
        functools.partial(back_kernel, factor),
        in_specs=[SMEM] + [VMEM] * (3 + 2 * PARTS),
        out_specs=[VMEM] * 5,
        out_shape=[
            jax.ShapeDtypeStruct((1, tokens), F32),
            jax.ShapeDtypeStruct((pieces, TOKENS_PIECE, COLS_PIECE), BF16),
        ]
        + [jax.ShapeDtypeStruct((tokens, e - c), BF16) for c, e in thirds(vocab)],
        compiler_params=params(16),
        cost_estimate=cost(4 * tokens * half * vocab, 4 * half * vocab),
        name="back_part",
    )(row, parts, draft, target, *weights)


def sum_kernel(terms, out):
    total = terms[0].astype(F32)
    for i in range(1, terms.shape[0]):
        total = total + terms[i].astype(F32)
    out[...] = jnp.broadcast_to(total.astype(BF16)[None], out.shape)


def sum_part(terms):
    return pl.pallas_call(
        sum_kernel,
        in_specs=[VMEM],
        out_specs=VMEM,
        out_shape=jax.ShapeDtypeStruct(terms.shape, BF16),
        compiler_params=params(8),
        name="sum_part",
    )(terms)


def join_kernel(pieces, out, stage, sems):
    tokens, width = out.shape
    down = tokens // TOKENS_PIECE
    steps = sems.shape[0]
    copies = []
    for step in range(steps):
        rows = pl.ds(step * tokens // steps, tokens // steps)
        for i in range(step * down // steps, (step + 1) * down // steps):
            for j in range(width // COLS_PIECE):
                place = pl.ds(i * TOKENS_PIECE, TOKENS_PIECE), pl.ds(j * COLS_PIECE, COLS_PIECE)
                stage[place] = pieces[j * down + i].astype(F32)
        copies.append(pltpu.make_async_copy(stage.at[rows], out.at[rows], sems.at[step]))
        copies[-1].start()
    for copy in copies:
        copy.wait()


def join_part(pieces, tokens, width):
    return pl.pallas_call(
        join_kernel,
        in_specs=[VMEM],
        out_specs=ANY,
        out_shape=jax.ShapeDtypeStruct((tokens, width), F32),
        scratch_shapes=[pltpu.VMEM((tokens, width), F32), pltpu.SemaphoreType.DMA((4,))],
        compiler_params=params(8),
        name="join_part",
    )(pieces)


def head_kernel(mine, *rest):
    dlogits, (mine_o, *dlogits_o), (out, held, *held_o, stage, sems, out_sems) = rest[:3], rest[3:7], rest[7:]
    steps, step = stage.shape[:2]
    pairs = zip((mine_o, *dlogits_o), (held, *held_o))
    loads = [pltpu.make_async_copy(*pair, sems.at[i]) for i, pair in enumerate(pairs)]
    for each in loads:
        each.start()
    copies = []
    for j in range(steps):
        part = pl.ds(j * step, step)
        for i, (c, e) in enumerate(thirds(out.shape[1])):
            value = dot(mine[:, part], dlogits[i][...], 0, 0)
            if j == 0:
                for each in (loads[:2] if i == 0 else loads[i + 1 : i + 2]):
                    each.wait()
            stage[j, :, c:e] = value + dot(held[:, part], held_o[i][...], 0, 0)
        copies.append(pltpu.make_async_copy(stage.at[j], out.at[part], out_sems.at[j]))
        copies[-1].start()
    for copy in copies:
        copy.wait()


def head_part(mine, mine_o, dlogits, dlogits_o):
    tokens, half = mine.shape
    vocab = sum(x.shape[1] for x in dlogits)
    step = 128
    return pl.pallas_call(
        head_kernel,
        in_specs=[VMEM] * 4 + [ANY] * 4,
        out_specs=ANY,
        out_shape=jax.ShapeDtypeStruct((half, vocab), F32),
        scratch_shapes=[pltpu.VMEM(x.shape, BF16) for x in (mine_o, *dlogits_o)]
        + [
            pltpu.VMEM((half // step, step, vocab), F32),
            pltpu.SemaphoreType.DMA((4,)),
            pltpu.SemaphoreType.DMA((half // step,)),
        ],
        compiler_params=params(24),
        cost_estimate=cost(4 * tokens * half * vocab, 4 * half * vocab),
        name="head_part",
    )(mine, *dlogits, mine_o, *dlogits_o)


def shards(hidden, weight, target):
    n = lax.axis_size("vocab")
    row = jnp.full((1,), lax.axis_index("rows"), jnp.int32)
    tokens, width = hidden.shape
    half, vocab = weight.shape

    with jax.named_scope("swap_hidden"):
        hidden_o = swap(hidden)
    split = 2 * BLOCK
    first = cross_part(row, hidden_o, weight, 0, split)
    second = cross_part(row, hidden_o, weight, split, vocab)
    with jax.named_scope("swap_draft"):
        first, second = swap(first), swap(second)
    acc, probs, stat, *weights = own_part(row, hidden, target, weight)
    hidden, acc = lax.optimization_barrier((hidden, acc))
    mine = lax.dynamic_slice_in_dim(hidden, row[0] * half, half, 1)
    theirs = lax.dynamic_slice_in_dim(hidden, (1 - row[0]) * half, half, 1)
    first, second, acc, *weights = lax.optimization_barrier((first, second, acc, *weights))
    with jax.named_scope("swap_weight"):
        weights_o = [swap(x) for x in weights]
    draft, part = draft_part(acc, probs, stat, first, second)
    with jax.named_scope("share_stats"):
        parts = lax.all_to_all(jnp.broadcast_to(part[None], (n,) + part.shape), "vocab", 0, 0)
    divergence, pieces, *dlogits = back_part(
        vocab * n / 1024.0, row, parts, draft, target, [*weights, *weights_o]
    )
    with jax.named_scope("scatter_sum"):
        terms = lax.all_to_all(pieces, "vocab", 0, 0)
    with jax.named_scope("swap_dlogits"):
        mine_o, dlogits_o = swap(theirs), [swap(x) for x in dlogits]
    head_grad = head_part(mine, mine_o, dlogits, dlogits_o)
    terms, head_grad = lax.optimization_barrier((terms, head_grad))
    totals = sum_part(terms)
    with jax.named_scope("gather"):
        gathered = lax.all_to_all(totals, "vocab", 0, 0)
    hidden_grad = join_part(gathered, tokens, width)
    return (divergence.reshape(tokens), hidden_grad, head_grad)


def solution(mesh):
    return jax.shard_map(
        shards,
        mesh=mesh,
        in_specs=(P("rows", None), P("rows", "vocab"), P("rows", "vocab")),
        out_specs=(P("rows"), P("rows", None), P("rows", "vocab")),
        check_vma=False,
    )
```

```python
import functools
import math
import jax
import jax.numpy as jnp
from jax import lax
from jax.experimental import pallas as pl
from jax.experimental.pallas import tpu as pltpu
from jax.sharding import PartitionSpec as P

SWAP = ((0, 1), (1, 0))
TOKENS_PIECE = 16
COLS_PIECE = 512
GROUP = 64
LOG2E = math.log2(math.e)
F32, BF16 = jnp.float32, jnp.bfloat16
VMEM = pl.BlockSpec(memory_space=pltpu.VMEM)
HBM = pl.BlockSpec(memory_space=pltpu.HBM)
ANY = pl.BlockSpec(memory_space=pl.ANY)


def dot(a, b, ca, cb):
    return lax.dot_general(a, b, (((ca,), (cb,)), ((), ())), preferred_element_type=F32)


def swap(x):
    return lax.ppermute(x, "rows", SWAP)


def params(mib):
    return pltpu.CompilerParams(vmem_limit_bytes=mib * 1024 * 1024)


def cost(flops, moved):
    return pl.CostEstimate(flops=flops, bytes_accessed=moved, transcendentals=0)


def exp(x):
    return jnp.exp2(x * LOG2E)


def thirds(n):
    step = pl.cdiv(n // 128, 3) * 128
    return [(c, min(c + step, n)) for c in range(0, n, step)]


def stat_rows(tokens):
    return pl.cdiv(3 * tokens // 128, 8) * 8


def own_kernel(mine, target, weight, acc, probs, stat, buffer, sem):
    copy = pltpu.make_async_copy(weight, buffer, sem)
    copy.start()
    wide = target[...].astype(F32)
    peak = jnp.max(wide, axis=1, keepdims=True)
    terms = exp(wide - peak)
    total = jnp.sum(terms, axis=1, keepdims=True)
    terms = terms / total
    probs[...] = terms
    mean = jnp.sum(terms * wide, axis=1, keepdims=True)
    lane = lax.broadcasted_iota(jnp.int32, stat.shape, 1)
    stat[...] = jnp.where(lane == 0, peak + jnp.log(total), mean)
    copy.wait()
    acc[...] = dot(mine[...], buffer[...], 1, 0)


def own_part(mine, target, weight):
    tokens, half = mine.shape
    vocab = target.shape[1]
    return pl.pallas_call(
        own_kernel,
        in_specs=[VMEM] * 2 + [ANY],
        out_specs=[VMEM] * 4,
        out_shape=[
            jax.ShapeDtypeStruct((tokens, vocab), F32),
            jax.ShapeDtypeStruct((tokens, vocab), F32),
            jax.ShapeDtypeStruct((tokens, 128), F32),
            jax.ShapeDtypeStruct((half, vocab), BF16),
        ],
        scratch_shapes=[pltpu.SemaphoreType.DMA],
        compiler_params=params(16),
        cost_estimate=cost(2 * tokens * half * vocab, 2 * half * vocab),
        name="own_part",
    )(mine, target, weight)


def draft_kernel(theirs, acc, probs, stat, weight, draft, out, buffer, sem):
    tokens, vocab = draft.shape
    copy = pltpu.make_async_copy(weight, buffer, sem)
    copy.start()
    copy.wait()
    draft[...] = acc[...] + dot(theirs[...], buffer[...], 1, 0)
    lse_q, mean = [], []
    for first in range(0, tokens, GROUP):
        rows = slice(first, first + GROUP)
        peak = jnp.full((GROUP, 128), -jnp.inf, F32)
        cross = jnp.zeros((GROUP, 128), F32)
        for t in range(0, vocab, 128):
            value = draft[rows, t : t + 128]
            peak = jnp.maximum(peak, value)
            cross = cross + probs[rows, t : t + 128] * value
        top = jnp.max(peak, axis=1, keepdims=True)
        total = jnp.zeros((GROUP, 128), F32)
        for t in range(0, vocab, 128):
            total = total + exp(draft[rows, t : t + 128] - top)
        lse_q.append(top + jnp.log(jnp.sum(total, axis=1, keepdims=True)))
        mean.append(stat[rows, 1:2] - jnp.sum(cross, axis=1, keepdims=True))
    lse_q, mean = jnp.concatenate(lse_q, axis=0), jnp.concatenate(mean, axis=0)
    lane = lax.broadcasted_iota(jnp.int32, stat.shape, 1)
    rows = jnp.where(lane == 0, stat[:, :1], jnp.where(lane == 1, mean, lse_q)).T
    out[...] = jnp.zeros(out.shape, F32)
    for i in range(3):
        for k in range(tokens // 128):
            at = i * (tokens // 128) + k
            out[at : at + 1] = rows[i : i + 1, k * 128 : (k + 1) * 128]


def draft_part(theirs, acc, probs, stat, weight):
    tokens, half = theirs.shape
    vocab = acc.shape[1]
    return pl.pallas_call(
        draft_kernel,
        in_specs=[VMEM] * 4 + [ANY],
        out_specs=[VMEM] * 3,
        out_shape=[
            jax.ShapeDtypeStruct((tokens, vocab), F32),
            jax.ShapeDtypeStruct((stat_rows(tokens), 128), F32),
            jax.ShapeDtypeStruct((half, vocab), BF16),
        ],
        scratch_shapes=[pltpu.SemaphoreType.DMA],
        compiler_params=params(20),
        cost_estimate=cost(2 * tokens * half * vocab, 2 * half * vocab),
        name="draft_part",
    )(theirs, acc, probs, stat, weight)


def back_kernel(factor, row, parts, draft, target, weight, weight_o, divergence, out, *dlogits):
    lines = draft.shape[0] // 128
    every = parts[...]
    top = jnp.max(every, axis=0)
    scale = exp(every - top)
    lse = top + jnp.log(jnp.sum(scale, axis=0))
    cross = jnp.sum(scale[:, :lines] * every[:, lines : 2 * lines], axis=0)
    mean = cross / jnp.sum(scale[:, :lines], axis=0)
    result = mean - lse[:lines] + lse[2 * lines : 3 * lines]
    for k in range(lines):
        divergence[:, k * 128 : (k + 1) * 128] = result[k : k + 1]
    turned = jnp.concatenate([lse, jnp.zeros((128 - lse.shape[0], 128), F32)], axis=0).T
    lse_t = jnp.concatenate([turned[:, k : k + 1] for k in range(lines)], axis=0)
    lse_q = jnp.concatenate([turned[:, 2 * lines + k : 2 * lines + k + 1] for k in range(lines)], axis=0)

    half = weight.shape[0]
    per = half // COLS_PIECE
    down = draft.shape[0] // TOKENS_PIECE
    sums = [None] * (2 * per)
    for kept, (c, e) in zip(dlogits, thirds(draft.shape[1])):
        probs_q = exp(draft[:, c:e] - lse_q)
        probs_t = exp(target[:, c:e].astype(F32) - lse_t)
        block = ((probs_q - probs_t) * factor).astype(BF16)
        kept[...] = block
        for j in range(2 * per):
            rows = pl.ds(j % per * COLS_PIECE, COLS_PIECE)
            term = dot(block, (weight, weight_o)[j // per][rows, c:e], 1, 1)
            sums[j] = term if sums[j] is None else sums[j] + term
    for j in range(2 * per):
        place = lax.rem(row[0] * per + j, 2 * per)
        out[pl.ds(place * down, down)] = sums[j].astype(BF16).reshape(down, TOKENS_PIECE, COLS_PIECE)


def back_part(factor, row, parts, draft, target, weight, weight_o):
    tokens, vocab = draft.shape
    half = weight.shape[0]
    pieces = (tokens // TOKENS_PIECE) * (2 * half // COLS_PIECE)
    return pl.pallas_call(
        functools.partial(back_kernel, factor),
        in_specs=[pl.BlockSpec(memory_space=pltpu.SMEM)] + [VMEM] * 5,
        out_specs=[VMEM] * 5,
        out_shape=[
            jax.ShapeDtypeStruct((1, tokens), F32),
            jax.ShapeDtypeStruct((pieces, TOKENS_PIECE, COLS_PIECE), BF16),
        ]
        + [jax.ShapeDtypeStruct((tokens, e - c), BF16) for c, e in thirds(vocab)],
        compiler_params=params(16),
        cost_estimate=cost(4 * tokens * half * vocab, 4 * half * vocab),
        name="back_part",
    )(row, parts, draft, target, weight, weight_o)


def sum_kernel(terms, out):
    total = terms[0].astype(F32)
    for i in range(1, terms.shape[0]):
        total = total + terms[i].astype(F32)
    out[...] = jnp.broadcast_to(total.astype(BF16)[None], out.shape)


def sum_part(terms):
    return pl.pallas_call(
        sum_kernel,
        in_specs=[VMEM],
        out_specs=VMEM,
        out_shape=jax.ShapeDtypeStruct(terms.shape, BF16),
        compiler_params=params(8),
        name="sum_part",
    )(terms)


def join_kernel(pieces, out, stage, sems):
    tokens, width = out.shape
    down = tokens // TOKENS_PIECE
    steps = sems.shape[0]
    copies = []
    for step in range(steps):
        rows = pl.ds(step * tokens // steps, tokens // steps)
        for i in range(step * down // steps, (step + 1) * down // steps):
            for j in range(width // COLS_PIECE):
                place = pl.ds(i * TOKENS_PIECE, TOKENS_PIECE), pl.ds(j * COLS_PIECE, COLS_PIECE)
                stage[place] = pieces[j * down + i].astype(F32)
        copies.append(pltpu.make_async_copy(stage.at[rows], out.at[rows], sems.at[step]))
        copies[-1].start()
    for copy in copies:
        copy.wait()


def join_part(pieces, tokens, width):
    return pl.pallas_call(
        join_kernel,
        in_specs=[VMEM],
        out_specs=ANY,
        out_shape=jax.ShapeDtypeStruct((tokens, width), F32),
        scratch_shapes=[pltpu.VMEM((tokens, width), F32), pltpu.SemaphoreType.DMA((4,))],
        compiler_params=params(8),
        name="join_part",
    )(pieces)


def head_kernel(mine, *rest):
    dlogits, (mine_o, *dlogits_o), (out, held, *held_o, stage, sems, out_sems) = rest[:3], rest[3:7], rest[7:]
    steps, step = stage.shape[:2]
    pairs = zip((mine_o, *dlogits_o), (held, *held_o))
    loads = [pltpu.make_async_copy(*pair, sems.at[i]) for i, pair in enumerate(pairs)]
    for each in loads:
        each.start()
    copies = []
    for j in range(steps):
        part = pl.ds(j * step, step)
        for i, (c, e) in enumerate(thirds(out.shape[1])):
            value = dot(mine[:, part], dlogits[i][...], 0, 0)
            if j == 0:
                for each in (loads[:2] if i == 0 else loads[i + 1 : i + 2]):
                    each.wait()
            stage[j, :, c:e] = value + dot(held[:, part], held_o[i][...], 0, 0)
        copies.append(pltpu.make_async_copy(stage.at[j], out.at[part], out_sems.at[j]))
        copies[-1].start()
    for copy in copies:
        copy.wait()


def head_part(mine, mine_o, dlogits, dlogits_o):
    tokens, half = mine.shape
    vocab = sum(x.shape[1] for x in dlogits)
    step = 128
    return pl.pallas_call(
        head_kernel,
        in_specs=[VMEM] * 4 + [ANY] * 4,
        out_specs=ANY,
        out_shape=jax.ShapeDtypeStruct((half, vocab), F32),
        scratch_shapes=[pltpu.VMEM(x.shape, BF16) for x in (mine_o, *dlogits_o)]
        + [
            pltpu.VMEM((half // step, step, vocab), F32),
            pltpu.SemaphoreType.DMA((4,)),
            pltpu.SemaphoreType.DMA((half // step,)),
        ],
        compiler_params=params(24),
        cost_estimate=cost(4 * tokens * half * vocab, 4 * half * vocab),
        name="head_part",
    )(mine, *dlogits, mine_o, *dlogits_o)


def shards(hidden, weight, target):
    n = lax.axis_size("vocab")
    row = lax.axis_index("rows")
    tokens, width = hidden.shape
    half, vocab = weight.shape

    with jax.named_scope("swap_weight"):
        weight_o = swap(weight)
    mine = lax.dynamic_slice_in_dim(hidden, row * half, half, 1)
    theirs = lax.dynamic_slice_in_dim(hidden, (1 - row) * half, half, 1)

    acc, probs, stat, weight_v = own_part(mine, target, weight)
    draft, part, weight_o = draft_part(theirs, acc, probs, stat, weight_o)
    with jax.named_scope("share_stats"):
        parts = lax.all_to_all(jnp.broadcast_to(part[None], (n,) + part.shape), "vocab", 0, 0)
    divergence, pieces, *dlogits = back_part(
        vocab * n / 1024.0, jnp.full((1,), row, jnp.int32), parts, draft, target, weight_v, weight_o
    )
    with jax.named_scope("scatter_sum"):
        terms = lax.all_to_all(pieces, "vocab", 0, 0)
    with jax.named_scope("swap_back"):
        mine_o, dlogits_o = swap(theirs), [swap(x) for x in dlogits]
    head_grad = head_part(mine, mine_o, dlogits, dlogits_o)
    terms, head_grad = lax.optimization_barrier((terms, head_grad))
    totals = sum_part(terms)
    with jax.named_scope("gather"):
        gathered = lax.all_to_all(totals, "vocab", 0, 0)
    hidden_grad = join_part(gathered, tokens, width)
    return (divergence.reshape(tokens), hidden_grad, head_grad)


def solution(mesh):
    return jax.shard_map(
        shards,
        mesh=mesh,
        in_specs=(P("rows", None), P("rows", "vocab"), P("rows", "vocab")),
        out_specs=(P("rows"), P("rows", None), P("rows", "vocab")),
        check_vma=False,
    )
```

```python
import functools
import math
import jax
import jax.numpy as jnp
from jax import lax
from jax.experimental import pallas as pl
from jax.experimental.pallas import tpu as pltpu
from jax.sharding import PartitionSpec as P

SWAP = ((0, 1), (1, 0))
TOKENS_PIECE = 16
COLS_PIECE = 512
GROUP = 64
LOG2E = math.log2(math.e)
F32, BF16 = jnp.float32, jnp.bfloat16
VMEM = pl.BlockSpec(memory_space=pltpu.VMEM)
HBM = pl.BlockSpec(memory_space=pltpu.HBM)
ANY = pl.BlockSpec(memory_space=pl.ANY)


def dot(a, b, ca, cb):
    return lax.dot_general(a, b, (((ca,), (cb,)), ((), ())), preferred_element_type=F32)


def swap(x):
    return lax.ppermute(x, "rows", SWAP)


def params(mib):
    return pltpu.CompilerParams(vmem_limit_bytes=mib * 1024 * 1024)


def cost(flops, moved):
    return pl.CostEstimate(flops=flops, bytes_accessed=moved, transcendentals=0)


def exp(x):
    return jnp.exp2(x * LOG2E)


def thirds(n):
    step = pl.cdiv(n // 128, 3) * 128
    return [(c, min(c + step, n)) for c in range(0, n, step)]


def stat_rows(tokens):
    return pl.cdiv(3 * tokens // 128, 8) * 8


def own_kernel(mine, target, weight, acc, probs, stat, buffer, sem):
    copy = pltpu.make_async_copy(weight, buffer, sem)
    copy.start()
    wide = target[...].astype(F32)
    peak = jnp.max(wide, axis=1, keepdims=True)
    terms = exp(wide - peak)
    total = jnp.sum(terms, axis=1, keepdims=True)
    terms = terms / total
    probs[...] = terms
    mean = jnp.sum(terms * wide, axis=1, keepdims=True)
    lane = lax.broadcasted_iota(jnp.int32, stat.shape, 1)
    stat[...] = jnp.where(lane == 0, peak + jnp.log(total), mean)
    copy.wait()
    acc[...] = dot(mine[...], buffer[...], 1, 0)


def own_part(mine, target, weight):
    tokens, half = mine.shape
    vocab = target.shape[1]
    return pl.pallas_call(
        own_kernel,
        in_specs=[VMEM] * 2 + [ANY],
        out_specs=[VMEM] * 4,
        out_shape=[
            jax.ShapeDtypeStruct((tokens, vocab), F32),
            jax.ShapeDtypeStruct((tokens, vocab), F32),
            jax.ShapeDtypeStruct((tokens, 128), F32),
            jax.ShapeDtypeStruct((half, vocab), BF16),
        ],
        scratch_shapes=[pltpu.SemaphoreType.DMA],
        compiler_params=params(16),
        cost_estimate=cost(2 * tokens * half * vocab, 2 * half * vocab),
        name="own_part",
    )(mine, target, weight)


def draft_kernel(theirs, acc, probs, stat, weight, draft, out, buffer, sems):
    tokens, vocab = draft.shape
    copies = []
    for j, (c, e) in enumerate(thirds(vocab)):
        part = pl.ds(c, e - c)
        copies.append(pltpu.make_async_copy(weight.at[:, part], buffer.at[:, part], sems.at[j]))
        copies[-1].start()
    for copy, (c, e) in zip(copies, thirds(vocab)):
        copy.wait()
        draft[:, c:e] = acc[:, c:e] + dot(theirs[...], buffer[:, c:e], 1, 0)
    lse_q, mean = [], []
    for first in range(0, tokens, GROUP):
        rows = slice(first, first + GROUP)
        peak = jnp.full((GROUP, 128), -jnp.inf, F32)
        cross = jnp.zeros((GROUP, 128), F32)
        for t in range(0, vocab, 128):
            value = draft[rows, t : t + 128]
            peak = jnp.maximum(peak, value)
            cross = cross + probs[rows, t : t + 128] * value
        top = jnp.max(peak, axis=1, keepdims=True)
        total = jnp.zeros((GROUP, 128), F32)
        for t in range(0, vocab, 128):
            total = total + exp(draft[rows, t : t + 128] - top)
        lse_q.append(top + jnp.log(jnp.sum(total, axis=1, keepdims=True)))
        mean.append(stat[rows, 1:2] - jnp.sum(cross, axis=1, keepdims=True))
    lse_q, mean = jnp.concatenate(lse_q, axis=0), jnp.concatenate(mean, axis=0)
    lane = lax.broadcasted_iota(jnp.int32, stat.shape, 1)
    rows = jnp.where(lane == 0, stat[:, :1], jnp.where(lane == 1, mean, lse_q)).T
    out[...] = jnp.zeros(out.shape, F32)
    for i in range(3):
        for k in range(tokens // 128):
            at = i * (tokens // 128) + k
            out[at : at + 1] = rows[i : i + 1, k * 128 : (k + 1) * 128]


def draft_part(theirs, acc, probs, stat, weight):
    tokens, half = theirs.shape
    vocab = acc.shape[1]
    return pl.pallas_call(
        draft_kernel,
        in_specs=[VMEM] * 4 + [ANY],
        out_specs=[VMEM] * 3,
        out_shape=[
            jax.ShapeDtypeStruct((tokens, vocab), F32),
            jax.ShapeDtypeStruct((stat_rows(tokens), 128), F32),
            jax.ShapeDtypeStruct((half, vocab), BF16),
        ],
        scratch_shapes=[pltpu.SemaphoreType.DMA((3,))],
        compiler_params=params(20),
        cost_estimate=cost(2 * tokens * half * vocab, 2 * half * vocab),
        name="draft_part",
    )(theirs, acc, probs, stat, weight)


def back_kernel(factor, row, parts, draft, target, weight, weight_o, divergence, out, *dlogits):
    lines = draft.shape[0] // 128
    every = parts[...]
    top = jnp.max(every, axis=0)
    scale = exp(every - top)
    lse = top + jnp.log(jnp.sum(scale, axis=0))
    cross = jnp.sum(scale[:, :lines] * every[:, lines : 2 * lines], axis=0)
    mean = cross / jnp.sum(scale[:, :lines], axis=0)
    result = mean - lse[:lines] + lse[2 * lines : 3 * lines]
    for k in range(lines):
        divergence[:, k * 128 : (k + 1) * 128] = result[k : k + 1]
    turned = jnp.concatenate([lse, jnp.zeros((128 - lse.shape[0], 128), F32)], axis=0).T
    lse_t = jnp.concatenate([turned[:, k : k + 1] for k in range(lines)], axis=0)
    lse_q = jnp.concatenate([turned[:, 2 * lines + k : 2 * lines + k + 1] for k in range(lines)], axis=0)

    half = weight.shape[0]
    per = half // COLS_PIECE
    down = draft.shape[0] // TOKENS_PIECE
    sums = [None] * (2 * per)
    for kept, (c, e) in zip(dlogits, thirds(draft.shape[1])):
        probs_q = exp(draft[:, c:e] - lse_q)
        probs_t = exp(target[:, c:e].astype(F32) - lse_t)
        block = ((probs_q - probs_t) * factor).astype(BF16)
        kept[...] = block
        for j in range(2 * per):
            rows = pl.ds(j % per * COLS_PIECE, COLS_PIECE)
            term = dot(block, (weight, weight_o)[j // per][rows, c:e], 1, 1)
            sums[j] = term if sums[j] is None else sums[j] + term
    for j in range(2 * per):
        place = lax.rem(row[0] * per + j, 2 * per)
        out[pl.ds(place * down, down)] = sums[j].astype(BF16).reshape(down, TOKENS_PIECE, COLS_PIECE)


def back_part(factor, row, parts, draft, target, weight, weight_o):
    tokens, vocab = draft.shape
    half = weight.shape[0]
    pieces = (tokens // TOKENS_PIECE) * (2 * half // COLS_PIECE)
    return pl.pallas_call(
        functools.partial(back_kernel, factor),
        in_specs=[pl.BlockSpec(memory_space=pltpu.SMEM)] + [VMEM] * 5,
        out_specs=[VMEM] * 5,
        out_shape=[
            jax.ShapeDtypeStruct((1, tokens), F32),
            jax.ShapeDtypeStruct((pieces, TOKENS_PIECE, COLS_PIECE), BF16),
        ]
        + [jax.ShapeDtypeStruct((tokens, e - c), BF16) for c, e in thirds(vocab)],
        compiler_params=params(16),
        cost_estimate=cost(4 * tokens * half * vocab, 4 * half * vocab),
        name="back_part",
    )(row, parts, draft, target, weight, weight_o)


def sum_kernel(terms, out):
    total = terms[0].astype(F32)
    for i in range(1, terms.shape[0]):
        total = total + terms[i].astype(F32)
    out[...] = jnp.broadcast_to(total.astype(BF16)[None], out.shape)


def sum_part(terms):
    return pl.pallas_call(
        sum_kernel,
        in_specs=[VMEM],
        out_specs=VMEM,
        out_shape=jax.ShapeDtypeStruct(terms.shape, BF16),
        compiler_params=params(8),
        name="sum_part",
    )(terms)


def join_kernel(pieces, out, stage, sems):
    tokens, width = out.shape
    down = tokens // TOKENS_PIECE
    steps = sems.shape[0]
    copies = []
    for step in range(steps):
        rows = pl.ds(step * tokens // steps, tokens // steps)
        for i in range(step * down // steps, (step + 1) * down // steps):
            for j in range(width // COLS_PIECE):
                place = pl.ds(i * TOKENS_PIECE, TOKENS_PIECE), pl.ds(j * COLS_PIECE, COLS_PIECE)
                stage[place] = pieces[j * down + i].astype(F32)
        copies.append(pltpu.make_async_copy(stage.at[rows], out.at[rows], sems.at[step]))
        copies[-1].start()
    for copy in copies:
        copy.wait()


def join_part(pieces, tokens, width):
    return pl.pallas_call(
        join_kernel,
        in_specs=[VMEM],
        out_specs=ANY,
        out_shape=jax.ShapeDtypeStruct((tokens, width), F32),
        scratch_shapes=[pltpu.VMEM((tokens, width), F32), pltpu.SemaphoreType.DMA((4,))],
        compiler_params=params(8),
        name="join_part",
    )(pieces)


def head_kernel(mine, *rest):
    dlogits, (mine_o, *dlogits_o), (out, held, *held_o, stage, sems, out_sems) = rest[:3], rest[3:7], rest[7:]
    steps, step = stage.shape[:2]
    pairs = zip((mine_o, *dlogits_o), (held, *held_o))
    loads = [pltpu.make_async_copy(*pair, sems.at[i]) for i, pair in enumerate(pairs)]
    for each in loads:
        each.start()
    copies = []
    for j in range(steps):
        part = pl.ds(j * step, step)
        for i, (c, e) in enumerate(thirds(out.shape[1])):
            value = dot(mine[:, part], dlogits[i][...], 0, 0)
            if j == 0:
                for each in (loads[:2] if i == 0 else loads[i + 1 : i + 2]):
                    each.wait()
            stage[j, :, c:e] = value + dot(held[:, part], held_o[i][...], 0, 0)
        copies.append(pltpu.make_async_copy(stage.at[j], out.at[part], out_sems.at[j]))
        copies[-1].start()
    for copy in copies:
        copy.wait()


def head_part(mine, mine_o, dlogits, dlogits_o):
    tokens, half = mine.shape
    vocab = sum(x.shape[1] for x in dlogits)
    step = 128
    return pl.pallas_call(
        head_kernel,
        in_specs=[VMEM] * 4 + [ANY] * 4,
        out_specs=ANY,
        out_shape=jax.ShapeDtypeStruct((half, vocab), F32),
        scratch_shapes=[pltpu.VMEM(x.shape, BF16) for x in (mine_o, *dlogits_o)]
        + [
            pltpu.VMEM((half // step, step, vocab), F32),
            pltpu.SemaphoreType.DMA((4,)),
            pltpu.SemaphoreType.DMA((half // step,)),
        ],
        compiler_params=params(24),
        cost_estimate=cost(4 * tokens * half * vocab, 4 * half * vocab),
        name="head_part",
    )(mine, *dlogits, mine_o, *dlogits_o)


def shards(hidden, weight, target):
    n = lax.axis_size("vocab")
    row = lax.axis_index("rows")
    tokens, width = hidden.shape
    half, vocab = weight.shape

    with jax.named_scope("swap_weight"):
        weight_o = swap(weight)
    mine = lax.dynamic_slice_in_dim(hidden, row * half, half, 1)
    theirs = lax.dynamic_slice_in_dim(hidden, (1 - row) * half, half, 1)

    acc, probs, stat, weight_v = own_part(mine, target, weight)
    draft, part, weight_o = draft_part(theirs, acc, probs, stat, weight_o)
    with jax.named_scope("share_stats"):
        parts = lax.all_to_all(jnp.broadcast_to(part[None], (n,) + part.shape), "vocab", 0, 0)
    divergence, pieces, *dlogits = back_part(
        vocab * n / 1024.0, jnp.full((1,), row, jnp.int32), parts, draft, target, weight_v, weight_o
    )
    with jax.named_scope("scatter_sum"):
        terms = lax.all_to_all(pieces, "vocab", 0, 0)
    with jax.named_scope("swap_back"):
        mine_o, dlogits_o = swap(theirs), [swap(x) for x in dlogits]
    head_grad = head_part(mine, mine_o, dlogits, dlogits_o)
    terms, head_grad = lax.optimization_barrier((terms, head_grad))
    totals = sum_part(terms)
    with jax.named_scope("gather"):
        gathered = lax.all_to_all(totals, "vocab", 0, 0)
    hidden_grad = join_part(gathered, tokens, width)
    return (divergence.reshape(tokens), hidden_grad, head_grad)


def solution(mesh):
    return jax.shard_map(
        shards,
        mesh=mesh,
        in_specs=(P("rows", None), P("rows", "vocab"), P("rows", "vocab")),
        out_specs=(P("rows"), P("rows", None), P("rows", "vocab")),
        check_vma=False,
    )
```

```python
import functools
import math
import jax
import jax.numpy as jnp
from jax import lax
from jax.experimental import pallas as pl
from jax.experimental.pallas import tpu as pltpu
from jax.sharding import PartitionSpec as P

SWAP = ((0, 1), (1, 0))
TOKENS_PIECE = 16
COLS_PIECE = 512
GROUP = 64
LOG2E = math.log2(math.e)
F32, BF16 = jnp.float32, jnp.bfloat16
VMEM = pl.BlockSpec(memory_space=pltpu.VMEM)
HBM = pl.BlockSpec(memory_space=pltpu.HBM)
ANY = pl.BlockSpec(memory_space=pl.ANY)


def dot(a, b, ca, cb):
    return lax.dot_general(a, b, (((ca,), (cb,)), ((), ())), preferred_element_type=F32)


def swap(x):
    return lax.ppermute(x, "rows", SWAP)


def params(mib):
    return pltpu.CompilerParams(vmem_limit_bytes=mib * 1024 * 1024)


def cost(flops, moved):
    return pl.CostEstimate(flops=flops, bytes_accessed=moved, transcendentals=0)


def exp(x):
    return jnp.exp2(x * LOG2E)


def thirds(n):
    step = pl.cdiv(n // 128, 3) * 128
    return [(c, min(c + step, n)) for c in range(0, n, step)]


def stat_rows(tokens):
    return pl.cdiv(3 * tokens // 128, 8) * 8


def own_kernel(mine, target, weight, acc, probs, stat, buffer, sem):
    copy = pltpu.make_async_copy(weight, buffer, sem)
    copy.start()
    wide = target[...].astype(F32)
    peak = jnp.max(wide, axis=1, keepdims=True)
    terms = exp(wide - peak)
    total = jnp.sum(terms, axis=1, keepdims=True)
    terms = terms / total
    probs[...] = terms
    mean = jnp.sum(terms * wide, axis=1, keepdims=True)
    lane = lax.broadcasted_iota(jnp.int32, stat.shape, 1)
    stat[...] = jnp.where(lane == 0, peak + jnp.log(total), mean)
    copy.wait()
    acc[...] = dot(mine[...], buffer[...], 1, 0)


def own_part(mine, target, weight):
    tokens, half = mine.shape
    vocab = target.shape[1]
    return pl.pallas_call(
        own_kernel,
        in_specs=[VMEM] * 2 + [ANY],
        out_specs=[VMEM] * 4,
        out_shape=[
            jax.ShapeDtypeStruct((tokens, vocab), F32),
            jax.ShapeDtypeStruct((tokens, vocab), F32),
            jax.ShapeDtypeStruct((tokens, 128), F32),
            jax.ShapeDtypeStruct((half, vocab), BF16),
        ],
        scratch_shapes=[pltpu.SemaphoreType.DMA],
        compiler_params=params(16),
        cost_estimate=cost(2 * tokens * half * vocab, 2 * half * vocab),
        name="own_part",
    )(mine, target, weight)


def draft_kernel(theirs, acc, probs, stat, weight, draft, out, buffer, sems):
    tokens, vocab = draft.shape
    copies = []
    for j, (c, e) in enumerate(thirds(vocab)):
        part = pl.ds(c, e - c)
        copies.append(pltpu.make_async_copy(weight.at[:, part], buffer.at[:, part], sems.at[j]))
        copies[-1].start()
    for copy, (c, e) in zip(copies, thirds(vocab)):
        copy.wait()
        draft[:, c:e] = acc[:, c:e] + dot(theirs[...], buffer[:, c:e], 1, 0)
    lse_q, mean = [], []
    for first in range(0, tokens, GROUP):
        rows = slice(first, first + GROUP)
        peak = jnp.full((GROUP, 128), -jnp.inf, F32)
        cross = jnp.zeros((GROUP, 128), F32)
        for t in range(0, vocab, 128):
            value = draft[rows, t : t + 128]
            peak = jnp.maximum(peak, value)
            cross = cross + probs[rows, t : t + 128] * value
        top = jnp.max(peak, axis=1, keepdims=True)
        total = jnp.zeros((GROUP, 128), F32)
        for t in range(0, vocab, 128):
            total = total + exp(draft[rows, t : t + 128] - top)
        lse_q.append(top + jnp.log(jnp.sum(total, axis=1, keepdims=True)))
        mean.append(stat[rows, 1:2] - jnp.sum(cross, axis=1, keepdims=True))
    lse_q, mean = jnp.concatenate(lse_q, axis=0), jnp.concatenate(mean, axis=0)
    lane = lax.broadcasted_iota(jnp.int32, stat.shape, 1)
    rows = jnp.where(lane == 0, stat[:, :1], jnp.where(lane == 1, mean, lse_q)).T
    out[...] = jnp.zeros(out.shape, F32)
    for i in range(3):
        for k in range(tokens // 128):
            at = i * (tokens // 128) + k
            out[at : at + 1] = rows[i : i + 1, k * 128 : (k + 1) * 128]


def draft_part(theirs, acc, probs, stat, weight):
    tokens, half = theirs.shape
    vocab = acc.shape[1]
    return pl.pallas_call(
        draft_kernel,
        in_specs=[VMEM] * 4 + [ANY],
        out_specs=[VMEM] * 3,
        out_shape=[
            jax.ShapeDtypeStruct((tokens, vocab), F32),
            jax.ShapeDtypeStruct((stat_rows(tokens), 128), F32),
            jax.ShapeDtypeStruct((half, vocab), BF16),
        ],
        scratch_shapes=[pltpu.SemaphoreType.DMA((3,))],
        compiler_params=params(20),
        cost_estimate=cost(2 * tokens * half * vocab, 2 * half * vocab),
        name="draft_part",
    )(theirs, acc, probs, stat, weight)


def back_kernel(factor, row, parts, draft, target, weight, weight_o, divergence, out, *rest):
    *dlogits, stage, sems = rest
    lines = draft.shape[0] // 128
    every = parts[...]
    top = jnp.max(every, axis=0)
    scale = exp(every - top)
    lse = top + jnp.log(jnp.sum(scale, axis=0))
    cross = jnp.sum(scale[:, :lines] * every[:, lines : 2 * lines], axis=0)
    mean = cross / jnp.sum(scale[:, :lines], axis=0)
    result = mean - lse[:lines] + lse[2 * lines : 3 * lines]
    for k in range(lines):
        divergence[:, k * 128 : (k + 1) * 128] = result[k : k + 1]
    turned = jnp.concatenate([lse, jnp.zeros((128 - lse.shape[0], 128), F32)], axis=0).T
    lse_t = jnp.concatenate([turned[:, k : k + 1] for k in range(lines)], axis=0)
    lse_q = jnp.concatenate([turned[:, 2 * lines + k : 2 * lines + k + 1] for k in range(lines)], axis=0)

    half = weight.shape[0]
    per = half // COLS_PIECE
    down = draft.shape[0] // TOKENS_PIECE
    sums, copies = [None] * (2 * per), []
    for kept, (c, e) in zip(dlogits, thirds(draft.shape[1])):
        probs_q = exp(draft[:, c:e] - lse_q)
        probs_t = exp(target[:, c:e].astype(F32) - lse_t)
        block = ((probs_q - probs_t) * factor).astype(BF16)
        kept[...] = block
        for j in range(2 * per):
            rows = pl.ds(j % per * COLS_PIECE, COLS_PIECE)
            term = dot(block, (weight, weight_o)[j // per][rows, c:e], 1, 1)
            sums[j] = term if sums[j] is None else sums[j] + term
            if e == draft.shape[1]:
                place = lax.rem(row[0] * per + j, 2 * per)
                stage[j] = sums[j].astype(BF16).reshape(down, TOKENS_PIECE, COLS_PIECE)
                copies.append(pltpu.make_async_copy(stage.at[j], out.at[pl.ds(place * down, down)], sems.at[j]))
                copies[-1].start()
    for copy in copies:
        copy.wait()


def back_part(factor, row, parts, draft, target, weight, weight_o):
    tokens, vocab = draft.shape
    half = weight.shape[0]
    pieces = (tokens // TOKENS_PIECE) * (2 * half // COLS_PIECE)
    return pl.pallas_call(
        functools.partial(back_kernel, factor),
        in_specs=[pl.BlockSpec(memory_space=pltpu.SMEM)] + [VMEM] * 5,
        out_specs=[VMEM, ANY] + [VMEM] * 3,
        out_shape=[
            jax.ShapeDtypeStruct((1, tokens), F32),
            jax.ShapeDtypeStruct((pieces, TOKENS_PIECE, COLS_PIECE), BF16),
        ]
        + [jax.ShapeDtypeStruct((tokens, e - c), BF16) for c, e in thirds(vocab)],
        scratch_shapes=[
            pltpu.VMEM((2 * half // COLS_PIECE, tokens // TOKENS_PIECE, TOKENS_PIECE, COLS_PIECE), BF16),
            pltpu.SemaphoreType.DMA((2 * half // COLS_PIECE,)),
        ],
        compiler_params=params(16),
        cost_estimate=cost(4 * tokens * half * vocab, 4 * half * vocab),
        name="back_part",
    )(row, parts, draft, target, weight, weight_o)


def sum_kernel(terms, out):
    total = terms[0].astype(F32)
    for i in range(1, terms.shape[0]):
        total = total + terms[i].astype(F32)
    out[...] = jnp.broadcast_to(total.astype(BF16)[None], out.shape)


def sum_part(terms):
    return pl.pallas_call(
        sum_kernel,
        in_specs=[VMEM],
        out_specs=VMEM,
        out_shape=jax.ShapeDtypeStruct(terms.shape, BF16),
        compiler_params=params(8),
        name="sum_part",
    )(terms)


def join_kernel(pieces, out, stage, sems):
    tokens, width = out.shape
    down = tokens // TOKENS_PIECE
    steps = sems.shape[0]
    copies = []
    for step in range(steps):
        rows = pl.ds(step * tokens // steps, tokens // steps)
        for i in range(step * down // steps, (step + 1) * down // steps):
            for j in range(width // COLS_PIECE):
                place = pl.ds(i * TOKENS_PIECE, TOKENS_PIECE), pl.ds(j * COLS_PIECE, COLS_PIECE)
                stage[place] = pieces[j * down + i].astype(F32)
        copies.append(pltpu.make_async_copy(stage.at[rows], out.at[rows], sems.at[step]))
        copies[-1].start()
    for copy in copies:
        copy.wait()


def join_part(pieces, tokens, width):
    return pl.pallas_call(
        join_kernel,
        in_specs=[VMEM],
        out_specs=ANY,
        out_shape=jax.ShapeDtypeStruct((tokens, width), F32),
        scratch_shapes=[pltpu.VMEM((tokens, width), F32), pltpu.SemaphoreType.DMA((4,))],
        compiler_params=params(8),
        name="join_part",
    )(pieces)


def head_kernel(mine, *rest):
    dlogits, (mine_o, *dlogits_o), (out, held, *held_o, stage, sems, out_sems) = rest[:3], rest[3:7], rest[7:]
    steps, step = stage.shape[:2]
    pairs = zip((mine_o, *dlogits_o), (held, *held_o))
    loads = [pltpu.make_async_copy(*pair, sems.at[i]) for i, pair in enumerate(pairs)]
    for each in loads:
        each.start()
    copies = []
    for j in range(steps):
        part = pl.ds(j * step, step)
        for i, (c, e) in enumerate(thirds(out.shape[1])):
            value = dot(mine[:, part], dlogits[i][...], 0, 0)
            if j == 0:
                for each in (loads[:2] if i == 0 else loads[i + 1 : i + 2]):
                    each.wait()
            stage[j, :, c:e] = value + dot(held[:, part], held_o[i][...], 0, 0)
        copies.append(pltpu.make_async_copy(stage.at[j], out.at[part], out_sems.at[j]))
        copies[-1].start()
    for copy in copies:
        copy.wait()


def head_part(mine, mine_o, dlogits, dlogits_o):
    tokens, half = mine.shape
    vocab = sum(x.shape[1] for x in dlogits)
    step = 128
    return pl.pallas_call(
        head_kernel,
        in_specs=[VMEM] * 4 + [ANY] * 4,
        out_specs=ANY,
        out_shape=jax.ShapeDtypeStruct((half, vocab), F32),
        scratch_shapes=[pltpu.VMEM(x.shape, BF16) for x in (mine_o, *dlogits_o)]
        + [
            pltpu.VMEM((half // step, step, vocab), F32),
            pltpu.SemaphoreType.DMA((4,)),
            pltpu.SemaphoreType.DMA((half // step,)),
        ],
        compiler_params=params(24),
        cost_estimate=cost(4 * tokens * half * vocab, 4 * half * vocab),
        name="head_part",
    )(mine, *dlogits, mine_o, *dlogits_o)


def shards(hidden, weight, target):
    n = lax.axis_size("vocab")
    row = lax.axis_index("rows")
    tokens, width = hidden.shape
    half, vocab = weight.shape

    with jax.named_scope("swap_weight"):
        weight_o = swap(weight)
    mine = lax.dynamic_slice_in_dim(hidden, row * half, half, 1)
    theirs = lax.dynamic_slice_in_dim(hidden, (1 - row) * half, half, 1)

    acc, probs, stat, weight_v = own_part(mine, target, weight)
    draft, part, weight_o = draft_part(theirs, acc, probs, stat, weight_o)
    with jax.named_scope("share_stats"):
        parts = lax.all_to_all(jnp.broadcast_to(part[None], (n,) + part.shape), "vocab", 0, 0)
    divergence, pieces, *dlogits = back_part(
        vocab * n / 1024.0, jnp.full((1,), row, jnp.int32), parts, draft, target, weight_v, weight_o
    )
    with jax.named_scope("scatter_sum"):
        terms = lax.all_to_all(pieces, "vocab", 0, 0)
    with jax.named_scope("swap_back"):
        mine_o, dlogits_o = swap(theirs), [swap(x) for x in dlogits]
    head_grad = head_part(mine, mine_o, dlogits, dlogits_o)
    terms, head_grad = lax.optimization_barrier((terms, head_grad))
    totals = sum_part(terms)
    with jax.named_scope("gather"):
        gathered = lax.all_to_all(totals, "vocab", 0, 0)
    hidden_grad = join_part(gathered, tokens, width)
    return (divergence.reshape(tokens), hidden_grad, head_grad)


def solution(mesh):
    return jax.shard_map(
        shards,
        mesh=mesh,
        in_specs=(P("rows", None), P("rows", "vocab"), P("rows", "vocab")),
        out_specs=(P("rows"), P("rows", None), P("rows", "vocab")),
        check_vma=False,
    )
```
